128 devices in a mesh: ctx: 16 (over z, x_hi, core), samp: 4 (over y), tp: 2 (over x_lo).
Axes of the slice: x: 4 (x_hi: 2, x_lo: 2; x = x_hi * 2 + x_lo), y: 4, z: 4, core: 2. Of those that a mesh axis runs over, the one named last changes fastest.
Arguments:
- queries: bfloat16 [64, 256, 6144], P(('ctx', 'samp'), None, 'tp'), may hold values from -4.5 to 4.5
- out_grad: bfloat16 [64, 256, 6144], P(('ctx', 'samp'), None, 'tp'), may hold values from -12 to 12
- answer_kv: bfloat16 [64, 256, 256], P(('ctx', 'samp')), may hold values from -4.5 to 4.5
- prompt_kv: bfloat16 [4, 1024, 256], P(None, 'ctx'), may hold values from -4.5 to 4.5
- answer_prompt: int32 [64], P(('ctx', 'samp')), may hold values from 0 to 3, as said below
- answer_len: int32 [64], P(('ctx', 'samp')), may hold values from 32 to 256
Outputs:
- query_grad: float32 [64, 256, 6144], P(('ctx', 'samp'), None, 'tp')
- answer_kv_grad: float32 [64, 256, 256], P(('ctx', 'samp'))
- prompt_kv_grad: float32 [4, 1024, 256], P(None, 'ctx')
The draws below stay inside these ranges and needn't reach their ends.
Inputs may be any that keep to these rules, and one draw needn't show every extreme that they name: `answer_prompt`: every one of the 4 prompts is continued by at least one answer.
All inputs are finite; a program needn't handle non-finite values.
Results may differ from the reference program's by a relative error of at most 0.02.
Values may be sent and summed in bfloat16 or wider, within the bound.
A program may use at most 192 MiB of HBM per device.

```python
import jax
import jax.numpy as jnp
from jax import lax

HEADS = 48
HD = 128
NP = 4
ALEN = 256
PLEN = 1024
ANSWERS = 64


def draw_queries(key, part):
    key = jax.random.fold_in(key, 1)
    full_shape = (ANSWERS, ALEN, HEADS * HD)
    values = jnp.clip(jax.random.normal(key, full_shape, jnp.float32), -4.5, 4.5)
    return values.astype(jnp.bfloat16)


def draw_prompt_kv(key, part):
    key = jax.random.fold_in(key, 2)
    full_shape = (NP, PLEN, 2 * HD)
    values = jnp.clip(jax.random.normal(key, full_shape, jnp.float32), -4.5, 4.5)
    return values.astype(jnp.bfloat16)


def draw_answer_len(key, part):
    key = jax.random.fold_in(key, 3)
    draw_key, order_key = jax.random.split(key)
    lengths = jax.random.randint(draw_key, (ANSWERS,), ALEN // 8, ALEN + 1)
    shuffled = jax.random.permutation(order_key, ANSWERS)
    lengths = lengths.at[shuffled[0]].set(ALEN).at[shuffled[1]].set(ALEN // 8)
    return lengths.astype(jnp.int32)


def draw_answer_prompt(key, part):
    key = jax.random.fold_in(key, 4)
    draw_key, order_key = jax.random.split(key)
    owners = jax.random.randint(draw_key, (ANSWERS,), 0, NP)
    shuffled = jax.random.permutation(order_key, ANSWERS)
    owners = owners.at[shuffled[:NP]].set(jnp.arange(NP, dtype=jnp.int32))
    return owners.astype(jnp.int32)


def steps_of(own_key, shape, shards, least, top_value):
    def one(axis_at, shards_of):
        heights = jax.random.uniform(jax.random.fold_in(jax.random.fold_in(own_key, 6), axis_at), (shards_of,), jnp.float32, least / len(shards), top_value / len(shards))
        return jnp.repeat(jnp.exp(heights), shape[axis_at] // shards_of).reshape((-1,) + (1,) * (len(shape) - axis_at - 1))

    loudness = one(*shards[0])
    for cut in shards[1:]:
        loudness = loudness * one(*cut)
    return loudness


def bell_draw(rng, extent, scale, bound, pieces=(), kind=jnp.bfloat16):
    factor_of = steps_of(rng, extent, pieces, -0.22, 0.18) if pieces else 1.0
    result = jax.random.normal(rng, extent, jnp.float32) * scale * factor_of
    return jnp.minimum(jnp.maximum(result, -bound), bound).astype(kind)


def setup_inputs(seed: int = 0) -> dict:
    arg_keys = jax.random.split(jax.random.key(seed), 7)
    return {
        "queries": draw_queries(jax.random.fold_in(arg_keys[6], 71), 0),
        "out_grad": bell_draw(arg_keys[1], (ANSWERS, ALEN, HEADS * HD), 2.0, 12.0, ((0, 64), (2, 2))),
        "answer_kv": bell_draw(arg_keys[2], (ANSWERS, ALEN, 2 * HD), 1.0, 4.5, ((0, 64),)),
        "prompt_kv": draw_prompt_kv(jax.random.fold_in(arg_keys[6], 71), 0),
        "answer_prompt": draw_answer_prompt(jax.random.fold_in(arg_keys[6], 71), 0),
        "answer_len": draw_answer_len(jax.random.fold_in(arg_keys[6], 71), 0),
    }


def reference(queries, out_grad, answer_kv, prompt_kv, answer_prompt, answer_len):
    score_scale = HD ** -0.5
    prompt_length = prompt_kv.shape[1]
    query_pos = jnp.arange(ALEN, dtype=jnp.int32)
    key_pos = jnp.arange(prompt_length + ALEN, dtype=jnp.int32)
    allowed = (key_pos[None, :] < prompt_length) | ((key_pos[None, :] - prompt_length) <= query_pos[:, None])

    def per_answer(accumulated, inputs):
        query, grad, own_kv, prompt, length = inputs
        chosen = lax.dynamic_index_in_dim(prompt_kv, prompt, 0, keepdims=False)
        key_rows = jnp.concatenate([chosen, own_kv], axis=0).astype(jnp.float32)
        key_part = key_rows[:, :HD]
        value_part = key_rows[:, HD:]
        q_heads = query.reshape(ALEN, HEADS, HD).astype(jnp.float32)
        live_rows = query_pos < length
        grad_in = jnp.where(live_rows[:, None], grad, jnp.zeros_like(grad))
        g_heads = grad_in.reshape(ALEN, HEADS, HD).astype(jnp.float32)
        scores = jnp.einsum("thd,kd->thk", q_heads, key_part) * score_scale
        scores = jnp.where(allowed[:, None, :], scores, -jnp.inf)
        row_top = jnp.max(scores, axis=-1, keepdims=True)
        weights = jnp.exp(scores - row_top)
        probs = weights / jnp.sum(weights, axis=-1, keepdims=True)
        probs_b = probs.astype(jnp.bfloat16)
        dprobs = jnp.einsum("thd,kd->thk", g_heads, value_part)
        row_delta = jnp.sum(probs_b.astype(jnp.float32) * dprobs, axis=-1, keepdims=True)
        dscores_b = (probs * (dprobs - row_delta)).astype(jnp.bfloat16)
        query_part = jnp.einsum("thk,kd->thd", dscores_b.astype(jnp.float32), key_part) * score_scale
        key_grad = jnp.einsum("thk,thd->kd", dscores_b.astype(jnp.float32), q_heads) * score_scale
        value_grad = jnp.einsum("thk,thd->kd", probs_b.astype(jnp.float32), g_heads)
        kv_grad = jnp.concatenate([key_grad, value_grad], axis=-1)
        current = lax.dynamic_index_in_dim(accumulated, prompt, 0, keepdims=False)
        accumulated = lax.dynamic_update_index_in_dim(accumulated, current + kv_grad[:prompt_length], prompt, 0)
        return accumulated, (query_part.reshape(ALEN, HEADS * HD), kv_grad[prompt_length:])

    zero_grads = jnp.zeros(prompt_kv.shape, jnp.float32)
    accumulated, outputs = lax.scan(per_answer, zero_grads, (queries, out_grad, answer_kv, answer_prompt, answer_len))
    return (outputs[0], outputs[1], accumulated)
```

```python
import functools

import jax
import jax.numpy as jnp
from jax import lax
from jax.experimental import pallas as pl
from jax.experimental.pallas import tpu as pltpu
from jax.sharding import PartitionSpec as P

BF = jnp.bfloat16
F32 = jnp.float32
T = 256
D = 128
PK = 1024
NK = PK + T
NP = 4
NC = 16
BL = PK // NC
NG = 8
SCALE = D**-0.5
EXP2 = SCALE * 1.4426950408889634
RC = 32
MESH = pl.DeviceIdType.MESH
VM = pl.BlockSpec(memory_space=pltpu.VMEM)
SM = pl.BlockSpec(memory_space=pltpu.SMEM)


def one_hot_tile(prompt):
    rows = lax.broadcasted_iota(jnp.int32, (8, 128), 0)
    return jnp.where(rows == prompt, 1.0, 0.0).astype(F32)


def weight_row(tile, prompt):
    row = tile[prompt : prompt + 1, :]
    return jnp.concatenate([row, row], axis=1)


def gather_kernel(ap_ref, kv_ref, out_ref, hot_ref, hot_send, send_buf, hs, hr, ds, dr):
    me = lax.axis_index("ctx")
    barrier = pltpu.get_barrier_semaphore()
    for i in range(1, NC):
        pl.semaphore_signal(
            barrier, inc=1, device_id={"ctx": lax.rem(me + i, NC)}, device_id_type=MESH
        )
    tile = one_hot_tile(ap_ref[0])
    hot_send[...] = tile
    hot_ref[me] = tile
    pl.semaphore_wait(barrier, NC - 1)

    def hot_copy(i):
        return pltpu.make_async_remote_copy(
            src_ref=hot_send,
            dst_ref=hot_ref.at[me],
            send_sem=hs.at[i],
            recv_sem=hr.at[i],
            device_id={"ctx": lax.rem(me + i, NC)},
            device_id_type=MESH,
        )

    def block_copy(i):
        return pltpu.make_async_remote_copy(
            src_ref=send_buf.at[i],
            dst_ref=out_ref.at[me],
            send_sem=ds.at[i],
            recv_sem=dr.at[i],
            device_id={"ctx": lax.rem(me + i, NC)},
            device_id_type=MESH,
        )

    for i in range(1, NC):
        hot_copy(i).start()

    def chosen(weights):
        total = kv_ref[0].astype(F32) * weight_row(weights, 0)
        for p in range(1, NP):
            total = total + kv_ref[p].astype(F32) * weight_row(weights, p)
        return total.astype(BF)

    out_ref[me] = chosen(tile)
    for i in range(1, NC):
        hot_copy(NC - i).wait_recv()
        send_buf[i] = chosen(hot_ref[lax.rem(me + i, NC)])
        block_copy(i).start()
    for i in range(1, NC):
        hot_copy(i).wait_send()
        block_copy(i).wait()


def gather(answer_prompt, prompt_kv):
    dma = pltpu.SemaphoreType.DMA((NC,))
    return pl.pallas_call(
        gather_kernel,
        out_shape=(
            jax.ShapeDtypeStruct((NC, BL, 2 * D), BF),
            jax.ShapeDtypeStruct((NC, 8, 128), F32),
        ),
        in_specs=[SM, VM],
        out_specs=(VM, VM),
        scratch_shapes=[pltpu.VMEM((8, 128), F32), pltpu.VMEM((NC, BL, 2 * D), BF), dma, dma, dma, dma],
        compiler_params=pltpu.CompilerParams(collective_id=0, has_side_effects=True),
        name="gather_prompt",
    )(answer_prompt, prompt_kv)


def head_cols(h):
    return pl.ds(pl.multiple_of(h * D, D), D)


def head_rows(h):
    return pl.ds(pl.multiple_of(h * T, T), T)


def prepare(h, q_ref, g_ref, gm, qt, gt, live):
    rows = lax.broadcasted_iota(jnp.int32, (T, D), 0)
    g = jnp.where(rows < live, g_ref[:, head_cols(h)].astype(F32), 0.0).astype(BF)
    gm[:, head_cols(h)] = g
    qt[:, head_rows(h)] = q_ref[:, head_cols(h)].T
    gt[:, head_rows(h)] = g.T


def products(h, q_ref, gm, kt, vt, s_buf, d_buf):
    s_buf[...] = jnp.dot(q_ref[:, head_cols(h)], kt[...], preferred_element_type=F32)
    d_buf[...] = jnp.dot(gm[:, head_cols(h)], vt[...], preferred_element_type=F32)


def softmax_terms(h, s_buf, d_buf, probs, dscores):
    for r in range(T // RC):
        r0 = r * RC
        width = PK + (128 if r0 < 128 else 256)
        rows = slice(r0, r0 + RC)
        out_rows = pl.ds(pl.multiple_of(h * T + r0, RC), RC)
        s = s_buf[rows, :width]
        row = lax.broadcasted_iota(jnp.int32, (RC, 128), 0) + (r0 % 128)
        col = lax.broadcasted_iota(jnp.int32, (RC, 128), 1)
        last = jnp.where(row >= col, s[:, width - 128 :], -jnp.inf)
        s = jnp.concatenate([s[:, : width - 128], last], axis=1)
        top = jnp.max(s, axis=1, keepdims=True)
        e = jnp.exp2((s - top) * EXP2)
        p = e * (1.0 / jnp.sum(e, axis=1, keepdims=True))
        probs[out_rows, :width] = p.astype(BF)
        d = d_buf[rows, :width]
        delta = jnp.sum(p * d, axis=1, keepdims=True)
        dscores[out_rows, :width] = (p * (d - delta)).astype(BF)
        if width < NK:
            probs[out_rows, width:] = jnp.zeros((RC, NK - width), BF)
            dscores[out_rows, width:] = jnp.zeros((RC, NK - width), BF)


def compute_kernel(
    heads, len_ref, q_ref, g_ref, pkv_ref, akv_ref, dq, dpkv, dakv,
    s0, s1, d0, d1, probs, dscores, qt, gt, gm, kt, vt, keys,
):
    live = len_ref[0]
    kt[:, :PK] = pkv_ref[:, :D].T
    vt[:, :PK] = pkv_ref[:, D:].T
    kt[:, PK:] = akv_ref[:, :D].T
    vt[:, PK:] = akv_ref[:, D:].T
    keys[:PK, :] = pkv_ref[:, :D]
    keys[PK:, :] = akv_ref[:, :D]

    def query_out(h):
        dq[:, head_cols(h)] = (
            jnp.dot(dscores[head_rows(h), :], keys[...], preferred_element_type=F32) * SCALE
        )

    prepare(0, q_ref, g_ref, gm, qt, gt, live)
    products(0, q_ref, gm, kt, vt, s0, d0)

    def step(h, now, later):
        after = jnp.minimum(h + 1, heads - 1)
        prepare(after, q_ref, g_ref, gm, qt, gt, live)
        products(after, q_ref, gm, kt, vt, *later)
        softmax_terms(h, *now, probs, dscores)
        query_out(h)

    def two_heads(i, carry):
        step(2 * i, (s0, d0), (s1, d1))
        step(2 * i + 1, (s1, d1), (s0, d0))
        return carry

    lax.fori_loop(0, heads // 2, two_heads, 0)
    for j in range(NK // 256):
        at = slice(j * 256, (j + 1) * 256)
        key_grad = jnp.dot(qt[...], dscores[:, at], preferred_element_type=F32) * SCALE
        value_grad = jnp.dot(gt[...], probs[:, at], preferred_element_type=F32)
        if j * 256 < PK:
            dpkv[at, :D] = key_grad.T.astype(BF)
            dpkv[at, D:] = value_grad.T.astype(BF)
        else:
            dakv[:, :D] = key_grad.T.astype(BF)
            dakv[:, D:] = value_grad.T.astype(BF)


def compute(answer_len, q, g, pkv, akv):
    heads = q.shape[1] // D
    rows = heads * T
    scratch = (
        [pltpu.VMEM((T, NK), F32)] * 4
        + [pltpu.VMEM((rows, NK), BF)] * 2
        + [pltpu.VMEM((D, rows), BF)] * 2
        + [pltpu.VMEM((T, heads * D), BF)]
        + [pltpu.VMEM((D, NK), BF)] * 2
        + [pltpu.VMEM((NK, D), BF)]
    )
    return pl.pallas_call(
        functools.partial(compute_kernel, heads),
        out_shape=(
            jax.ShapeDtypeStruct((T, heads * D), F32),
            jax.ShapeDtypeStruct((PK, 2 * D), BF),
            jax.ShapeDtypeStruct((T, 2 * D), BF),
        ),
        in_specs=[SM, VM, VM, VM, VM],
        out_specs=(VM, VM, VM),
        scratch_shapes=scratch,
        compiler_params=pltpu.CompilerParams(vmem_limit_bytes=61 * 2**20),
        name="attention_backward",
    )(answer_len, q, g, pkv, akv)


def reduce_kernel(
    hot_ref, dp_ref, da_ref, prompt_out, answer_out,
    blocks, parts, part_in, total, totals, mate, s1, r1, s2, r2, s3, r3, sm, rm,
):
    me = lax.axis_index("ctx")
    samp = lax.axis_index("samp")
    tp = lax.axis_index("tp")
    mine = samp * 2 + tp

    def member(i):
        other = lax.rem(mine + i, NG)
        return {"samp": other // 2, "tp": lax.rem(other, 2)}

    barrier = pltpu.get_barrier_semaphore()
    for i in range(1, NC):
        pl.semaphore_signal(
            barrier, inc=1, device_id={"ctx": lax.rem(me + i, NC)}, device_id_type=MESH
        )
    for i in range(1, NG):
        pl.semaphore_signal(barrier, inc=1, device_id=member(i), device_id_type=MESH)
    pl.semaphore_wait(barrier, NC - 1 + NG - 1)

    def block_copy(i):
        return pltpu.make_async_remote_copy(
            src_ref=dp_ref.at[lax.rem(me + i, NC)],
            dst_ref=blocks.at[i],
            send_sem=s1.at[i],
            recv_sem=r1.at[i],
            device_id={"ctx": lax.rem(me + i, NC)},
            device_id_type=MESH,
        )

    def part_copy(i):
        return pltpu.make_async_remote_copy(
            src_ref=parts.at[lax.rem(mine + i, NG)],
            dst_ref=part_in.at[i],
            send_sem=s2.at[i],
            recv_sem=r2.at[i],
            device_id=member(i),
            device_id_type=MESH,
        )

    def total_copy(i):
        return pltpu.make_async_remote_copy(
            src_ref=total,
            dst_ref=totals.at[mine],
            send_sem=s3.at[i],
            recv_sem=r3.at[i],
            device_id=member(i),
            device_id_type=MESH,
        )

    mate_copy = pltpu.make_async_remote_copy(
        src_ref=da_ref,
        dst_ref=mate,
        send_sem=sm,
        recv_sem=rm,
        device_id={"tp": 1 - tp},
        device_id_type=MESH,
    )
    for i in range(1, NC):
        block_copy(i).start()
    mate_copy.start()

    def add_block(block, weights, sums):
        block = block.astype(F32)
        return [s + block * weight_row(weights, p) for p, s in enumerate(sums)]

    acc = total.shape[0] // NP
    for i in range(1, NC):
        block_copy(i).wait_recv()
    for m in range(0, NG, 2):
        at = slice(m * acc, (m + 2) * acc)
        sums = [jnp.zeros((2 * acc, 2 * D), F32)] * NP
        sums = add_block(dp_ref[me, at, :], hot_ref[me], sums)
        for i in range(1, NC):
            sums = add_block(blocks[i, at, :], hot_ref[lax.rem(me - i + NC, NC)], sums)
        parts[m] = jnp.concatenate([s[:acc] for s in sums], axis=0).astype(BF)
        parts[m + 1] = jnp.concatenate([s[acc:] for s in sums], axis=0).astype(BF)
    for i in range(1, NG):
        part_copy(i).start()
    mate_copy.wait_recv()
    answer_out[...] = da_ref[...].astype(F32) + mate[...].astype(F32)
    whole = parts[mine].astype(F32)
    for i in range(1, NG):
        part_copy(i).wait_recv()
        whole = whole + part_in[i].astype(F32)
    total[...] = whole
    totals[mine] = whole
    for i in range(1, NG):
        total_copy(i).start()
    for i in range(1, NG):
        total_copy(i).wait_recv()
    for m in range(NG):
        for p in range(NP):
            prompt_out[p, m * acc : (m + 1) * acc, :] = totals[m, p * acc : (p + 1) * acc, :]
    mate_copy.wait_send()
    for i in range(1, NC):
        block_copy(i).wait_send()
    for i in range(1, NG):
        part_copy(i).wait_send()
        total_copy(i).wait_send()


def reduce(hot, dpkv, dakv):
    dma = pltpu.SemaphoreType.DMA
    part_rows = NP * BL // NG
    return pl.pallas_call(
        reduce_kernel,
        out_shape=(
            jax.ShapeDtypeStruct((NP, BL, 2 * D), F32),
            jax.ShapeDtypeStruct((T, 2 * D), F32),
        ),
        in_specs=[VM, VM, VM],
        out_specs=(VM, VM),
        scratch_shapes=[
            pltpu.VMEM((NC, BL, 2 * D), BF),
            pltpu.VMEM((NG, part_rows, 2 * D), BF),
            pltpu.VMEM((NG, part_rows, 2 * D), BF),
            pltpu.VMEM((part_rows, 2 * D), F32),
            pltpu.VMEM((NG, part_rows, 2 * D), F32),
            pltpu.VMEM((T, 2 * D), BF),
            dma((NC,)), dma((NC,)), dma((NG,)), dma((NG,)), dma((NG,)), dma((NG,)),
            dma, dma,
        ],
        compiler_params=pltpu.CompilerParams(collective_id=1, has_side_effects=True),
        name="reduce_grads",
    )(hot, dpkv.reshape(NC, BL, 2 * D), dakv)


def body(queries, out_grad, answer_kv, prompt_kv, answer_prompt, answer_len):
    chosen, hot = gather(answer_prompt, prompt_kv)
    dq, dpkv, dakv = compute(
        answer_len, queries[0], out_grad[0], chosen.reshape(PK, 2 * D), answer_kv[0]
    )
    prompt_grad, answer_grad = reduce(hot, dpkv, dakv)
    return dq[None], answer_grad[None], prompt_grad


def solution(mesh):
    placed = (
        P(("ctx", "samp"), None, "tp"),
        P(("ctx", "samp"), None, "tp"),
        P(("ctx", "samp"), None, None),
        P(None, "ctx", None),
        P(("ctx", "samp")),
        P(("ctx", "samp")),
    )
    return jax.shard_map(
        body,
        mesh=mesh,
        in_specs=placed,
        out_specs=(
            P(("ctx", "samp"), None, "tp"),
            P(("ctx", "samp"), None, None),
            P(None, "ctx", None),
        ),
        check_vma=False,
    )
```

```python
import functools

import jax
import jax.numpy as jnp
from jax import lax
from jax.experimental import pallas as pl
from jax.experimental.pallas import tpu as pltpu
from jax.sharding import PartitionSpec as P

BF = jnp.bfloat16
F32 = jnp.float32
T = 256
D = 128
PK = 1024
NK = PK + T
NP = 4
NC = 16
BL = PK // NC
NG = 8
SCALE = D**-0.5
EXP2 = SCALE * 1.4426950408889634
RC = 32
MESH = pl.DeviceIdType.MESH
VM = pl.BlockSpec(memory_space=pltpu.VMEM)
SM = pl.BlockSpec(memory_space=pltpu.SMEM)


def one_hot_tile(prompt):
    rows = lax.broadcasted_iota(jnp.int32, (8, 128), 0)
    return jnp.where(rows == prompt, 1.0, 0.0).astype(F32)


def weight_row(tile, prompt):
    row = tile[prompt : prompt + 1, :]
    return jnp.concatenate([row, row], axis=1)


def head_cols(h):
    return pl.ds(pl.multiple_of(h * D, D), D)


def head_rows(h):
    return pl.ds(pl.multiple_of(h * T, T), T)


def prepare(h, q_ref, g_ref, qt, gt, live):
    rows = lax.broadcasted_iota(jnp.int32, (T, D), 0)
    g = jnp.where(rows < live, g_ref[:, head_cols(h)].astype(F32), 0.0).astype(BF)
    g_ref[:, head_cols(h)] = g
    qt[:, head_rows(h)] = q_ref[:, head_cols(h)].T
    gt[:, head_rows(h)] = g.T


def products(h, q_ref, g_ref, kt, vt, s_buf, d_buf):
    s_buf[...] = jnp.dot(q_ref[:, head_cols(h)], kt[...], preferred_element_type=F32)
    d_buf[...] = jnp.dot(g_ref[:, head_cols(h)], vt[...], preferred_element_type=F32)


def softmax_terms(h, s_buf, d_buf, probs, dscores):
    for r in range(T // RC):
        r0 = r * RC
        width = PK + (128 if r0 < 128 else 256)
        rows = slice(r0, r0 + RC)
        out_rows = pl.ds(pl.multiple_of(h * T + r0, RC), RC)
        s = s_buf[rows, :width]
        row = lax.broadcasted_iota(jnp.int32, (RC, 128), 0) + (r0 % 128)
        col = lax.broadcasted_iota(jnp.int32, (RC, 128), 1)
        last = jnp.where(row >= col, s[:, width - 128 :], -jnp.inf)
        s = jnp.concatenate([s[:, : width - 128], last], axis=1)
        top = jnp.max(s, axis=1, keepdims=True)
        e = jnp.exp2((s - top) * EXP2)
        p = e * (1.0 / jnp.sum(e, axis=1, keepdims=True))
        probs[out_rows, :width] = p.astype(BF)
        d = d_buf[rows, :width]
        delta = jnp.sum(p * d, axis=1, keepdims=True)
        dscores[out_rows, :width] = (p * (d - delta)).astype(BF)
        if width < NK:
            probs[out_rows, width:] = jnp.zeros((RC, NK - width), BF)
            dscores[out_rows, width:] = jnp.zeros((RC, NK - width), BF)


CTX_STEPS = [(dz, dx, dc) for dz in (2, 1, 3, 0) for dx in (1, 0) for dc in (1, 0)]
OWN = len(CTX_STEPS) - 1
SAMP_STEPS = (2, 1, 3, 0)
MEMBERS = [(dy, dt) for dy in (2, 1, 3, 0) for dt in (1, 0)][:-1]
HEADS_AT_ONCE = 2
PIECE = BL // 4


def fused_kernel(
    heads, len_ref, ap_ref, q_hbm, g_hbm, akv_ref, pkv_ref,
    dq_hbm, prompt_out, answer_out,
    q_ref, g_ref, qt, gt, kt, vt, keys, s0, s1, d0, d1, probs, dscores, dq_buf,
    hot, hot_all, pick, chosen, grads, land, part, parts, mine_kv, mate_kv,
    load_sem, dq_sem, hs, hr, ps, pr, ts, tr, bs, br, ms, mr, xs, xr,
):
    ctx = lax.axis_index("ctx")
    samp = lax.axis_index("samp")
    tp = lax.axis_index("tp")
    z = ctx // 4
    xh = lax.rem(ctx // 2, 2)
    core = lax.rem(ctx, 2)

    def ctx_at(dz, dx, dc):
        return lax.rem(z + dz, 4) * 4 + lax.rem(xh + dx, 2) * 2 + lax.rem(core + dc, 2)

    def tp_at(dx):
        return lax.rem(tp + dx, 2)

    def samp_at(dy):
        return lax.rem(samp + dy, 4)

    def at(dz, dx, dc, dy=0):
        return {"ctx": ctx_at(dz, dx, dc), "samp": samp_at(dy), "tp": tp_at(dx)}

    def member(dy, dt):
        return {"samp": samp_at(dy), "tp": tp_at(dt)}

    barrier = pltpu.get_barrier_semaphore()
    for step in CTX_STEPS[:OWN]:
        pl.semaphore_signal(barrier, inc=1, device_id=at(*step), device_id_type=MESH)
    for dy, dt in MEMBERS:
        pl.semaphore_signal(barrier, inc=1, device_id=member(dy, dt), device_id_type=MESH)
    q_load = pltpu.make_async_copy(q_hbm, q_ref, load_sem.at[0])
    g_load = pltpu.make_async_copy(g_hbm, g_ref, load_sem.at[1])
    q_load.start()
    g_load.start()

    live = len_ref[0]
    tile = one_hot_tile(ap_ref[0])
    hot[OWN] = tile
    kt[:, PK:] = akv_ref[:, :D].T
    vt[:, PK:] = akv_ref[:, D:].T
    keys[PK:, :] = akv_ref[:, :D]
    q_load.wait()
    g_load.wait()

    def prepare_heads(first, last):
        def one(h, carry):
            prepare(h, q_ref, g_ref, qt, gt, live)
            return carry

        lax.fori_loop(first, last, one, 0)

    prepare_heads(0, heads // 2)
    pl.semaphore_wait(barrier, OWN + len(MEMBERS))

    def hot_copy(k):
        return pltpu.make_async_remote_copy(
            src_ref=hot.at[OWN],
            dst_ref=hot.at[k],
            send_sem=hs.at[k],
            recv_sem=hr.at[k],
            device_id=at(*CTX_STEPS[k]),
            device_id_type=MESH,
        )

    for k in range(OWN):
        hot_copy(k).start()
    prepare_heads(heads // 2, heads)

    def pick_copy(k):
        return pltpu.make_async_remote_copy(
            src_ref=pick.at[k],
            dst_ref=chosen.at[ctx],
            send_sem=ps.at[k],
            recv_sem=pr.at[k],
            device_id=at(*CTX_STEPS[k]),
            device_id_type=MESH,
        )

    def choose(weights):
        total = pkv_ref[0].astype(F32) * weight_row(weights, 0)
        for p in range(1, NP):
            total = total + pkv_ref[p].astype(F32) * weight_row(weights, p)
        return total.astype(BF)

    def back(k):
        dz, dx, dc = CTX_STEPS[k]
        return CTX_STEPS.index(((4 - dz) % 4, dx, dc))

    for k in range(OWN):
        hot_copy(back(k)).wait_recv()
        pick[k] = choose(hot[back(k)])
        pick_copy(k).start()
    chosen[ctx] = choose(tile)

    def table_copy(i):
        return pltpu.make_async_remote_copy(
            src_ref=hot,
            dst_ref=hot_all.at[i],
            send_sem=ts.at[i],
            recv_sem=tr.at[i],
            device_id={"samp": samp_at(i)},
            device_id_type=MESH,
        )

    for i in (2, 1, 3):
        table_copy(i).start()
    for k in range(OWN):
        pick_copy(k).wait_recv()

    for c in range(NC):
        rows = slice(c * BL, (c + 1) * BL)
        keys[rows, :] = chosen[c, :, :D]
    for c in range(0, NC, 2):
        pair = jnp.concatenate([chosen[c], chosen[c + 1]], axis=0)
        rows = slice(c * BL, (c + 2) * BL)
        kt[:, rows] = pair[:, :D].T
        vt[:, rows] = pair[:, D:].T

    def dq_copy(h, slot):
        return pltpu.make_async_copy(
            dq_buf.at[slot], dq_hbm.at[:, head_cols(h)], dq_sem.at[slot]
        )

    def query_out(h, slot):
        dq_buf[slot] = (
            jnp.dot(dscores[head_rows(h), :], keys[...], preferred_element_type=F32) * SCALE
        )

    products(0, q_ref, g_ref, kt, vt, s0, d0)

    def step(h, i, slot, now, later):
        after = jnp.minimum(h + 1, heads - 1)
        products(after, q_ref, g_ref, kt, vt, *later)
        softmax_terms(h, *now, probs, dscores)

        @pl.when(i > 0)
        def _():
            dq_copy(h, slot).wait()

        query_out(h, slot)
        dq_copy(h, slot).start()

    def two_heads(i, carry):
        step(2 * i, i, 0, (s0, d0), (s1, d1))
        step(2 * i + 1, i, 1, (s1, d1), (s0, d0))
        return carry

    lax.fori_loop(0, heads // 2, two_heads, 0)

    def piece_copy(k, i):
        dz, dx, dc = CTX_STEPS[k]
        row = ctx_at(dz, dx, dc) * BL + samp_at(i) * PIECE
        return pltpu.make_async_remote_copy(
            src_ref=grads.at[pl.ds(pl.multiple_of(row, PIECE), PIECE)],
            dst_ref=land.at[k, i],
            send_sem=bs.at[k, i],
            recv_sem=br.at[k, i],
            device_id=at(dz, dx, dc, i),
            device_id_type=MESH,
        )

    def key_value_grads(columns):
        key_grad = jnp.dot(qt[...], dscores[:, columns], preferred_element_type=F32) * SCALE
        value_grad = jnp.dot(gt[...], probs[:, columns], preferred_element_type=F32)
        return key_grad.T.astype(BF), value_grad.T.astype(BF)

    for first in range(0, OWN, 4):
        start = pl.multiple_of(lax.rem(z + CTX_STEPS[first][0], 4) * 256, 256)
        key_grad, value_grad = key_value_grads(pl.ds(start, 256))
        grads[pl.ds(start, 256), :D] = key_grad
        grads[pl.ds(start, 256), D:] = value_grad
        for k in range(first, first + 4):
            for i in SAMP_STEPS:
                if (k, i) != (OWN, 0):
                    piece_copy(k, i).start()
    row = pl.multiple_of(ctx * BL + samp * PIECE, PIECE)
    land[OWN, 0] = grads[pl.ds(row, PIECE), :]

    key_grad, value_grad = key_value_grads(slice(PK, NK))
    mine_kv[:, :D] = key_grad
    mine_kv[:, D:] = value_grad
    mate_copy = pltpu.make_async_remote_copy(
        src_ref=mine_kv,
        dst_ref=mate_kv,
        send_sem=xs,
        recv_sem=xr,
        device_id={"tp": 1 - tp},
        device_id_type=MESH,
    )
    mate_copy.start()

    for i in (2, 1, 3):
        table_copy(i).wait_recv()
    hot_all[0] = hot[...]
    sums = [jnp.zeros((PIECE, 2 * D), F32)] * NP
    for k in range(NC):
        for i in SAMP_STEPS:
            if (k, i) != (OWN, 0):
                piece_copy(k, i).wait_recv()
        for i in SAMP_STEPS:
            block = land[k, i].astype(F32)
            weights = hot_all[i, k]
            sums = [s + block * weight_row(weights, p) for p, s in enumerate(sums)]
    here = samp * 2 + tp
    for p in range(NP):
        part[p * PIECE : (p + 1) * PIECE, :] = sums[p].astype(BF)
    parts[here] = part[...]

    def part_copy(i):
        return pltpu.make_async_remote_copy(
            src_ref=part,
            dst_ref=parts.at[here],
            send_sem=ms.at[i],
            recv_sem=mr.at[i],
            device_id=member(*MEMBERS[i]),
            device_id_type=MESH,
        )

    for i in range(len(MEMBERS)):
        part_copy(i).start()
    mate_copy.wait_recv()
    answer_out[...] = mine_kv[...].astype(F32) + mate_kv[...].astype(F32)
    for k in range(OWN):
        hot_copy(k).wait_send()
        pick_copy(k).wait_send()
    for i in (2, 1, 3):
        table_copy(i).wait_send()
    for k in range(NC):
        for i in SAMP_STEPS:
            if (k, i) != (OWN, 0):
                piece_copy(k, i).wait_send()
    mate_copy.wait_send()
    for slot in range(HEADS_AT_ONCE):
        dq_copy(slot, slot).wait()
    for i in range(len(MEMBERS)):
        part_copy(i).wait()
    for s in range(4):
        both = parts[2 * s].astype(F32) + parts[2 * s + 1].astype(F32)
        for p in range(NP):
            prompt_out[p, s * PIECE : (s + 1) * PIECE, :] = both[p * PIECE : (p + 1) * PIECE, :]


def backward(answer_len, answer_prompt, q, g, akv, pkv):
    heads = q.shape[1] // D
    rows = heads * T
    vmem = pltpu.VMEM
    dma = pltpu.SemaphoreType.DMA
    hbm = pl.BlockSpec(memory_space=pl.ANY)
    return pl.pallas_call(
        functools.partial(fused_kernel, heads),
        out_shape=(
            jax.ShapeDtypeStruct((T, heads * D), F32),
            jax.ShapeDtypeStruct((NP, BL, 2 * D), F32),
            jax.ShapeDtypeStruct((T, 2 * D), F32),
        ),
        in_specs=[SM, SM, hbm, hbm, VM, VM],
        out_specs=(hbm, VM, VM),
        scratch_shapes=[
            vmem((T, heads * D), BF),
            vmem((T, heads * D), BF),
            vmem((D, rows), BF),
            vmem((D, rows), BF),
            vmem((D, NK), BF),
            vmem((D, NK), BF),
            vmem((NK, D), BF),
            vmem((T, NK), F32),
            vmem((T, NK), F32),
            vmem((T, NK), F32),
            vmem((T, NK), F32),
            vmem((rows, NK), BF),
            vmem((rows, NK), BF),
            vmem((HEADS_AT_ONCE, T, D), F32),
            vmem((NC, 8, 128), F32),
            vmem((4, NC, 8, 128), F32),
            vmem((OWN, BL, 2 * D), BF),
            vmem((NC, BL, 2 * D), BF),
            vmem((PK, 2 * D), BF),
            vmem((NC, 4, PIECE, 2 * D), BF),
            vmem((NP * PIECE, 2 * D), BF),
            vmem((NG, NP * PIECE, 2 * D), BF),
            vmem((T, 2 * D), BF),
            vmem((T, 2 * D), BF),
            dma((2,)),
            dma((HEADS_AT_ONCE,)),
            dma((NC,)), dma((NC,)), dma((NC,)), dma((NC,)),
            dma((4,)), dma((4,)),
            dma((NC, 4)), dma((NC, 4)),
            dma((NG,)), dma((NG,)),
            dma, dma,
        ],
        compiler_params=pltpu.CompilerParams(
            collective_id=0, has_side_effects=True, vmem_limit_bytes=61 * 2**20
        ),
        name="attention_backward",
    )(answer_len, answer_prompt, q, g, akv, pkv)


def body(queries, out_grad, answer_kv, prompt_kv, answer_prompt, answer_len):
    dq, prompt_grad, answer_grad = backward(
        answer_len, answer_prompt, queries[0], out_grad[0], answer_kv[0], prompt_kv
    )
    return dq[None], answer_grad[None], prompt_grad


def solution(mesh):
    placed = (
        P(("ctx", "samp"), None, "tp"),
        P(("ctx", "samp"), None, "tp"),
        P(("ctx", "samp"), None, None),
        P(None, "ctx", None),
        P(("ctx", "samp")),
        P(("ctx", "samp")),
    )
    return jax.shard_map(
        body,
        mesh=mesh,
        in_specs=placed,
        out_specs=(
            P(("ctx", "samp"), None, "tp"),
            P(("ctx", "samp"), None, None),
            P(None, "ctx", None),
        ),
        check_vma=False,
    )
```

```python
import functools

import jax
import jax.numpy as jnp
from jax import lax
from jax.experimental import pallas as pl
from jax.experimental.pallas import tpu as pltpu
from jax.sharding import PartitionSpec as P

BF = jnp.bfloat16
F32 = jnp.float32
T = 256
D = 128
PK = 1024
NK = PK + T
NP = 4
NC = 16
BL = PK // NC
NG = 8
SCALE = D**-0.5
EXP2 = SCALE * 1.4426950408889634
RC = 32
MESH = pl.DeviceIdType.MESH
VM = pl.BlockSpec(memory_space=pltpu.VMEM)
SM = pl.BlockSpec(memory_space=pltpu.SMEM)


def one_hot_tile(prompt):
    rows = lax.broadcasted_iota(jnp.int32, (8, 128), 0)
    return jnp.where(rows == prompt, 1.0, 0.0).astype(F32)


def weight_row(tile, prompt):
    row = tile[prompt : prompt + 1, :]
    return jnp.concatenate([row, row], axis=1)


def head_cols(h):
    return pl.ds(pl.multiple_of(h * D, D), D)


def head_rows(h):
    return pl.ds(pl.multiple_of(h * T, T), T)


def prepare(h, q_ref, g_ref, qt, gt, live):
    rows = lax.broadcasted_iota(jnp.int32, (T, D), 0)
    g = jnp.where(rows < live, g_ref[:, head_cols(h)].astype(F32), 0.0).astype(BF)
    g_ref[:, head_cols(h)] = g
    qt[:, head_rows(h)] = q_ref[:, head_cols(h)].T
    gt[:, head_rows(h)] = g.T


def own_products(h, q_ref, g_ref, kt, vt, s_own, d_own, probs, dscores):
    s = jnp.dot(q_ref[:, head_cols(h)], kt[:, PK:], preferred_element_type=F32)
    row = lax.broadcasted_iota(jnp.int32, (T, T), 0)
    col = lax.broadcasted_iota(jnp.int32, (T, T), 1)
    s_own[h] = jnp.where(row >= col, s, -jnp.inf)
    d_own[h] = jnp.dot(g_ref[:, head_cols(h)], vt[:, PK:], preferred_element_type=F32)
    top_rows = pl.ds(pl.multiple_of(h * T, T), T // 2)
    probs[top_rows, PK + T // 2 :] = jnp.zeros((T // 2, T // 2), BF)
    dscores[top_rows, PK + T // 2 :] = jnp.zeros((T // 2, T // 2), BF)


def products(h, q_ref, g_ref, kt, vt, s_buf, d_buf):
    s_buf[...] = jnp.dot(q_ref[:, head_cols(h)], kt[:, :PK], preferred_element_type=F32)
    d_buf[...] = jnp.dot(g_ref[:, head_cols(h)], vt[:, :PK], preferred_element_type=F32)


def softmax_terms(h, s_buf, d_buf, s_own, d_own, probs, dscores):
    for r in range(T // RC):
        r0 = r * RC
        own = 128 if r0 < 128 else 256
        rows = slice(r0, r0 + RC)
        out_rows = pl.ds(pl.multiple_of(h * T + r0, RC), RC)
        s = jnp.concatenate([s_buf[rows, :], s_own[h, rows, :own]], axis=1)
        top = jnp.max(s, axis=1, keepdims=True)
        e = jnp.exp2((s - top) * EXP2)
        p = e * (1.0 / jnp.sum(e, axis=1, keepdims=True))
        probs[out_rows, : PK + own] = p.astype(BF)
        d = jnp.concatenate([d_buf[rows, :], d_own[h, rows, :own]], axis=1)
        delta = jnp.sum(p * d, axis=1, keepdims=True)
        dscores[out_rows, : PK + own] = (p * (d - delta)).astype(BF)


CTX_STEPS = [(dz, dx, dc) for dz in (2, 1, 3, 0) for dx in (1, 0) for dc in (1, 0)]
OWN = len(CTX_STEPS) - 1
SAMP_STEPS = (2, 1, 3, 0)
MEMBERS = [(dy, dt) for dy in (2, 1, 3, 0) for dt in (1, 0)][:-1]
GROUP = 4
PIECE = BL // 4


def fused_kernel(
    heads, len_ref, ap_ref, q_hbm, g_hbm, akv_ref, pkv_ref,
    dq_hbm, prompt_out, answer_out,
    q_ref, g_ref, qt, gt, kt, vt, keys, s0, s1, d0, d1, s_own, d_own, probs, dscores,
    hot, hot_all, pick, chosen, grads, land, part, parts, mine_kv, mate_kv,
    load_sem, dq_sem, hs, hr, ps, pr, ts, tr, bs, br, ms, mr, xs, xr,
):
    ctx = lax.axis_index("ctx")
    samp = lax.axis_index("samp")
    tp = lax.axis_index("tp")
    z = ctx // 4
    xh = lax.rem(ctx // 2, 2)
    core = lax.rem(ctx, 2)

    def ctx_at(dz, dx, dc):
        return lax.rem(z + dz, 4) * 4 + lax.rem(xh + dx, 2) * 2 + lax.rem(core + dc, 2)

    def tp_at(dx):
        return lax.rem(tp + dx, 2)

    def samp_at(dy):
        return lax.rem(samp + dy, 4)

    def at(dz, dx, dc, dy=0):
        return {"ctx": ctx_at(dz, dx, dc), "samp": samp_at(dy), "tp": tp_at(dx)}

    def member(dy, dt):
        return {"samp": samp_at(dy), "tp": tp_at(dt)}

    barrier = pltpu.get_barrier_semaphore()
    for step in CTX_STEPS[:OWN]:
        pl.semaphore_signal(barrier, inc=1, device_id=at(*step), device_id_type=MESH)
    for dy, dt in MEMBERS:
        pl.semaphore_signal(barrier, inc=1, device_id=member(dy, dt), device_id_type=MESH)
    q_load = pltpu.make_async_copy(q_hbm, q_ref, load_sem.at[0])
    g_load = pltpu.make_async_copy(g_hbm, g_ref, load_sem.at[1])
    q_load.start()
    g_load.start()

    live = len_ref[0]
    tile = one_hot_tile(ap_ref[0])
    hot[OWN] = tile
    pl.semaphore_wait(barrier, OWN + len(MEMBERS))

    def hot_copy(k):
        return pltpu.make_async_remote_copy(
            src_ref=hot.at[OWN],
            dst_ref=hot.at[k],
            send_sem=hs.at[k],
            recv_sem=hr.at[k],
            device_id=at(*CTX_STEPS[k]),
            device_id_type=MESH,
        )

    for k in range(OWN):
        hot_copy(k).start()
    kt[:, PK:] = akv_ref[:, :D].T
    vt[:, PK:] = akv_ref[:, D:].T
    keys[PK:, :] = akv_ref[:, :D]
    q_load.wait()
    g_load.wait()

    def prepare_heads(i, carry):
        for h in range(4):
            prepare(4 * i + h, q_ref, g_ref, qt, gt, live)
        return carry

    lax.fori_loop(0, heads // 4, prepare_heads, 0)

    def pick_copy(k):
        return pltpu.make_async_remote_copy(
            src_ref=pick.at[k],
            dst_ref=chosen.at[ctx],
            send_sem=ps.at[k],
            recv_sem=pr.at[k],
            device_id=at(*CTX_STEPS[k]),
            device_id_type=MESH,
        )

    def choose(weights):
        total = pkv_ref[0].astype(F32) * weight_row(weights, 0)
        for p in range(1, NP):
            total = total + pkv_ref[p].astype(F32) * weight_row(weights, p)
        return total.astype(BF)

    def back(k):
        dz, dx, dc = CTX_STEPS[k]
        return CTX_STEPS.index(((4 - dz) % 4, dx, dc))

    for k in range(OWN):
        hot_copy(back(k)).wait_recv()
        pick[k] = choose(hot[back(k)])
        pick_copy(k).start()
    chosen[ctx] = choose(tile)

    def table_copy(i):
        return pltpu.make_async_remote_copy(
            src_ref=hot,
            dst_ref=hot_all.at[i],
            send_sem=ts.at[i],
            recv_sem=tr.at[i],
            device_id={"samp": samp_at(i)},
            device_id_type=MESH,
        )

    for i in (2, 1, 3):
        table_copy(i).start()

    def own_heads(i, carry):
        for h in range(4):
            own_products(4 * i + h, q_ref, g_ref, kt, vt, s_own, d_own, probs, dscores)
        return carry

    lax.fori_loop(0, heads // 4, own_heads, 0)

    def arrange(first_ctx):
        pair = jnp.concatenate([chosen[first_ctx], chosen[first_ctx + 1]], axis=0)
        start = pl.multiple_of(first_ctx * BL, 2 * BL)
        keys[pl.ds(start, 2 * BL), :] = pair[:, :D]
        kt[:, pl.ds(start, 2 * BL)] = pair[:, :D].T
        vt[:, pl.ds(start, 2 * BL)] = pair[:, D:].T

    for k in (14, 12, 4, 6, 8, 10, 0, 2):
        for one in (k, k + 1):
            if one != OWN:
                pick_copy(one).wait_recv()
        dz, dx, _ = CTX_STEPS[k]
        sender = lax.rem(z + 4 - dz, 4) * 4 + lax.rem(xh + dx, 2) * 2
        arrange(sender)

    products(0, q_ref, g_ref, kt, vt, s0, d0)

    def step(h, now, later):
        after = jnp.minimum(h + 1, heads - 1)
        products(after, q_ref, g_ref, kt, vt, *later)
        softmax_terms(h, *now, s_own, d_own, probs, dscores)

    def two_heads(i, carry):
        step(2 * i, (s0, d0), (s1, d1))
        step(2 * i + 1, (s1, d1), (s0, d0))
        return carry

    lax.fori_loop(0, heads // 2, two_heads, 0)

    def piece_copy(k, i):
        dz, dx, dc = CTX_STEPS[k]
        row = ctx_at(dz, dx, dc) * BL + samp_at(i) * PIECE
        return pltpu.make_async_remote_copy(
            src_ref=grads.at[pl.ds(pl.multiple_of(row, PIECE), PIECE)],
            dst_ref=land.at[k, i],
            send_sem=bs.at[k, i],
            recv_sem=br.at[k, i],
            device_id=at(dz, dx, dc, i),
            device_id_type=MESH,
        )

    def key_value_grads(columns):
        key_grad = jnp.dot(qt[...], dscores[:, columns], preferred_element_type=F32) * SCALE
        value_grad = jnp.dot(gt[...], probs[:, columns], preferred_element_type=F32)
        return key_grad.T.astype(BF), value_grad.T.astype(BF)

    key_grad, value_grad = key_value_grads(slice(PK, NK))
    mine_kv[:, :D] = key_grad
    mine_kv[:, D:] = value_grad
    mate_copy = pltpu.make_async_remote_copy(
        src_ref=mine_kv,
        dst_ref=mate_kv,
        send_sem=xs,
        recv_sem=xr,
        device_id={"tp": 1 - tp},
        device_id_type=MESH,
    )
    mate_copy.start()

    for first in range(0, OWN, 4):
        start = pl.multiple_of(lax.rem(z + CTX_STEPS[first][0], 4) * 256, 256)
        key_grad, value_grad = key_value_grads(pl.ds(start, 256))
        grads[pl.ds(start, 256), :D] = key_grad
        grads[pl.ds(start, 256), D:] = value_grad
        for k in range(first, first + 4):
            for i in SAMP_STEPS:
                if (k, i) != (OWN, 0):
                    piece_copy(k, i).start()
    row = pl.multiple_of(ctx * BL + samp * PIECE, PIECE)
    land[OWN, 0] = grads[pl.ds(row, PIECE), :]

    groups = heads // GROUP
    width = GROUP * D

    def query_grads(i):
        out = (s0, s1, d0, d1)[i // 2]
        start = (i % 2) * width
        rows = slice(i * GROUP * T, (i + 1) * GROUP * T)
        grad = jnp.dot(dscores[rows, :], keys[...], preferred_element_type=F32) * SCALE
        for h in range(GROUP):
            out[:, start + h * D : start + (h + 1) * D] = grad[h * T : (h + 1) * T, :]
        return pltpu.make_async_copy(
            out.at[:, pl.ds(start, width)], dq_hbm.at[:, pl.ds(i * width, width)], dq_sem.at[i]
        )

    query_copies = [query_grads(i) for i in range(groups // 2)]
    for copy in query_copies:
        copy.start()
    for i in (2, 1, 3):
        table_copy(i).wait_recv()
    hot_all[0] = hot[...]
    sums = [jnp.zeros((PIECE, 2 * D), F32)] * NP
    for k in range(NC):
        for i in SAMP_STEPS:
            if (k, i) != (OWN, 0):
                piece_copy(k, i).wait_recv()
        for i in SAMP_STEPS:
            block = land[k, i].astype(F32)
            weights = hot_all[i, k]
            sums = [s + block * weight_row(weights, p) for p, s in enumerate(sums)]
    here = samp * 2 + tp
    for p in range(NP):
        part[p * PIECE : (p + 1) * PIECE, :] = sums[p].astype(BF)
    parts[here] = part[...]

    def part_copy(i):
        return pltpu.make_async_remote_copy(
            src_ref=part,
            dst_ref=parts.at[here],
            send_sem=ms.at[i],
            recv_sem=mr.at[i],
            device_id=member(*MEMBERS[i]),
            device_id_type=MESH,
        )

    for i in range(len(MEMBERS)):
        part_copy(i).start()
    for i in range(groups // 2, groups):
        copy = query_grads(i)
        copy.start()
        query_copies.append(copy)
    mate_copy.wait_recv()
    answer_out[...] = mine_kv[...].astype(F32) + mate_kv[...].astype(F32)
    for k in range(OWN):
        hot_copy(k).wait_send()
        pick_copy(k).wait_send()
    for i in (2, 1, 3):
        table_copy(i).wait_send()
    for k in range(NC):
        for i in SAMP_STEPS:
            if (k, i) != (OWN, 0):
                piece_copy(k, i).wait_send()
    mate_copy.wait_send()
    for copy in query_copies:
        copy.wait()
    for i in range(len(MEMBERS)):
        part_copy(i).wait()
    for s in range(4):
        both = parts[2 * s].astype(F32) + parts[2 * s + 1].astype(F32)
        for p in range(NP):
            prompt_out[p, s * PIECE : (s + 1) * PIECE, :] = both[p * PIECE : (p + 1) * PIECE, :]


def backward(answer_len, answer_prompt, q, g, akv, pkv):
    heads = q.shape[1] // D
    rows = heads * T
    vmem = pltpu.VMEM
    dma = pltpu.SemaphoreType.DMA
    hbm = pl.BlockSpec(memory_space=pl.ANY)
    return pl.pallas_call(
        functools.partial(fused_kernel, heads),
        out_shape=(
            jax.ShapeDtypeStruct((T, heads * D), F32),
            jax.ShapeDtypeStruct((NP, BL, 2 * D), F32),
            jax.ShapeDtypeStruct((T, 2 * D), F32),
        ),
        in_specs=[SM, SM, hbm, hbm, VM, VM],
        out_specs=(hbm, VM, VM),
        scratch_shapes=[
            vmem((T, heads * D), BF),
            vmem((T, heads * D), BF),
            vmem((D, rows), BF),
            vmem((D, rows), BF),
            vmem((D, NK), BF),
            vmem((D, NK), BF),
            vmem((NK, D), BF),
            vmem((T, PK), F32),
            vmem((T, PK), F32),
            vmem((T, PK), F32),
            vmem((T, PK), F32),
            vmem((heads, T, T), F32),
            vmem((heads, T, T), F32),
            vmem((rows, NK), BF),
            vmem((rows, NK), BF),
            vmem((NC, 8, 128), F32),
            vmem((4, NC, 8, 128), F32),
            vmem((OWN, BL, 2 * D), BF),
            vmem((NC, BL, 2 * D), BF),
            vmem((PK, 2 * D), BF),
            vmem((NC, 4, PIECE, 2 * D), BF),
            vmem((NP * PIECE, 2 * D), BF),
            vmem((NG, NP * PIECE, 2 * D), BF),
            vmem((T, 2 * D), BF),
            vmem((T, 2 * D), BF),
            dma((2,)),
            dma((heads // GROUP,)),
            dma((NC,)), dma((NC,)), dma((NC,)), dma((NC,)),
            dma((4,)), dma((4,)),
            dma((NC, 4)), dma((NC, 4)),
            dma((NG,)), dma((NG,)),
            dma, dma,
        ],
        compiler_params=pltpu.CompilerParams(
            collective_id=0, has_side_effects=True, vmem_limit_bytes=61 * 2**20
        ),
        name="attention_backward",
    )(answer_len, answer_prompt, q, g, akv, pkv)


def place_kernel(parts, *refs):
    count = len(parts)
    ins, outs, held = refs[:count], refs[count : 2 * count], refs[2 * count : 3 * count]
    in_sems, out_sems = refs[3 * count :]
    loads, stores = [], []
    for i in range(count):
        rows = ins[i].shape[0] // parts[i]
        for j in range(parts[i]):
            at = pl.ds(j * rows, rows)
            n = len(loads)
            loads.append(pltpu.make_async_copy(ins[i].at[at], held[i].at[at], in_sems.at[n]))
            stores.append(pltpu.make_async_copy(held[i].at[at], outs[i].at[at], out_sems.at[n]))
    for load in loads:
        load.start()
    for load, store in zip(loads, stores):
        load.wait()
        store.start()
    for store in stores:
        store.wait()


def place(parts, *arrays):
    hbm = pl.BlockSpec(memory_space=pl.ANY)
    return pl.pallas_call(
        functools.partial(place_kernel, parts),
        out_shape=tuple(jax.ShapeDtypeStruct(a.shape, a.dtype) for a in arrays),
        in_specs=[hbm] * len(arrays),
        out_specs=(hbm,) * len(arrays),
        scratch_shapes=[pltpu.VMEM(a.shape, a.dtype) for a in arrays]
        + [pltpu.SemaphoreType.DMA((sum(parts),))] * 2,
        compiler_params=pltpu.CompilerParams(vmem_limit_bytes=61 * 2**20),
        name="place_outputs",
    )(*arrays)


def body(queries, out_grad, answer_kv, prompt_kv, answer_prompt, answer_len):
    dq, prompt_grad, answer_grad = backward(
        answer_len, answer_prompt, queries[0], out_grad[0], answer_kv[0], prompt_kv
    )
    dq, answer_grad, prompt_grad = place((8, 1, 1), dq, answer_grad, prompt_grad)
    return dq[None], answer_grad[None], prompt_grad


def solution(mesh):
    placed = (
        P(("ctx", "samp"), None, "tp"),
        P(("ctx", "samp"), None, "tp"),
        P(("ctx", "samp"), None, None),
        P(None, "ctx", None),
        P(("ctx", "samp")),
        P(("ctx", "samp")),
    )
    return jax.shard_map(
        body,
        mesh=mesh,
        in_specs=placed,
        out_specs=(
            P(("ctx", "samp"), None, "tp"),
            P(("ctx", "samp"), None, None),
            P(None, "ctx", None),
        ),
        check_vma=False,
    )
```

```python
import functools

import jax
import jax.numpy as jnp
from jax import lax
from jax.experimental import pallas as pl
from jax.experimental.pallas import tpu as pltpu
from jax.sharding import PartitionSpec as P

BF = jnp.bfloat16
F32 = jnp.float32
T = 256
D = 128
PK = 1024
NK = PK + T
NP = 4
NC = 16
BL = PK // NC
NG = 8
SCALE = D**-0.5
EXP2 = SCALE * 1.4426950408889634
RC = 32
MESH = pl.DeviceIdType.MESH
VM = pl.BlockSpec(memory_space=pltpu.VMEM)
SM = pl.BlockSpec(memory_space=pltpu.SMEM)


def one_hot_tile(prompt):
    rows = lax.broadcasted_iota(jnp.int32, (8, 128), 0)
    return jnp.where(rows == prompt, 1.0, 0.0).astype(F32)


def weight_row(tile, prompt):
    row = tile[prompt : prompt + 1, :]
    return jnp.concatenate([row, row], axis=1)


def head_cols(h):
    return pl.ds(pl.multiple_of(h * D, D), D)


def head_rows(h):
    return pl.ds(pl.multiple_of(h * T, T), T)


def prepare(h, q_ref, g_ref, qt, gt, live):
    rows = lax.broadcasted_iota(jnp.int32, (T, D), 0)
    g = jnp.where(rows < live, g_ref[:, head_cols(h)].astype(F32), 0.0).astype(BF)
    g_ref[:, head_cols(h)] = g
    qt[:, head_rows(h)] = q_ref[:, head_cols(h)].T
    gt[:, head_rows(h)] = g.T


def scaled_halves(keys):
    scaled = keys.astype(F32) * EXP2
    high = scaled.astype(BF)
    low = (scaled - high.astype(F32)).astype(BF)
    return jnp.concatenate([high, low], axis=1)


def twice(q):
    return jnp.concatenate([q, q], axis=1)


def own_products(h, q_ref, g_ref, kt, vt, s_own, d_own, probs, dscores):
    s = jnp.dot(twice(q_ref[:, head_cols(h)]), kt[:, PK:], preferred_element_type=F32)
    row = lax.broadcasted_iota(jnp.int32, (T, T), 0)
    col = lax.broadcasted_iota(jnp.int32, (T, T), 1)
    s_own[h] = jnp.where(row >= col, s, -jnp.inf)
    d_own[h] = jnp.dot(g_ref[:, head_cols(h)], vt[:, PK:], preferred_element_type=F32)
    top_rows = pl.ds(pl.multiple_of(h * T, T), T // 2)
    probs[top_rows, PK + T // 2 :] = jnp.zeros((T // 2, T // 2), BF)
    dscores[top_rows, PK + T // 2 :] = jnp.zeros((T // 2, T // 2), BF)


def products(h, q_ref, g_ref, kt, vt, s_buf, d_buf):
    s_buf[...] = jnp.dot(twice(q_ref[:, head_cols(h)]), kt[:, :PK], preferred_element_type=F32)
    d_buf[...] = jnp.dot(g_ref[:, head_cols(h)], vt[:, :PK], preferred_element_type=F32)


def softmax_terms(h, s_buf, d_buf, s_own, d_own, probs, dscores):
    for r in range(T // RC):
        r0 = r * RC
        own = 128 if r0 < 128 else 256
        rows = slice(r0, r0 + RC)
        out_rows = pl.ds(pl.multiple_of(h * T + r0, RC), RC)
        s = jnp.concatenate([s_buf[rows, :], s_own[h, rows, :own]], axis=1)
        top = jnp.max(s, axis=1, keepdims=True)
        e = jnp.exp2(s - top)
        p = e * (1.0 / jnp.sum(e, axis=1, keepdims=True))
        probs[out_rows, : PK + own] = p.astype(BF)
        d = jnp.concatenate([d_buf[rows, :], d_own[h, rows, :own]], axis=1)
        delta = jnp.sum(p * d, axis=1, keepdims=True)
        dscores[out_rows, : PK + own] = (p * (d - delta)).astype(BF)


CTX_STEPS = [(dz, dx, dc) for dz in (2, 1, 3, 0) for dx in (1, 0) for dc in (1, 0)]
OWN = len(CTX_STEPS) - 1
SAMP_STEPS = (2, 1, 3, 0)
MEMBERS = [(dy, dt) for dy in (2, 1, 3, 0) for dt in (1, 0)][:-1]
UNROLL = 6
GROUP = 4
PIECE = BL // 4


def fused_kernel(
    heads, len_ref, ap_ref, q_hbm, g_hbm, akv_ref, pkv_ref,
    dq, prompt_out, answer_out,
    q_ref, g_ref, qt, gt, kt, vt, keys, d1, s_own, d_own, probs, dscores,
    hot, hot_all, pick, chosen, grads, land, part, parts, mine_kv, mate_kv,
    load_sem, hs, hr, ps, pr, ts, tr, bs, br, ms, mr, xs, xr,
):
    s0, s1, d0 = (dq.at[:, pl.ds(i * PK, PK)] for i in range(3))
    ctx = lax.axis_index("ctx")
    samp = lax.axis_index("samp")
    tp = lax.axis_index("tp")
    z = ctx // 4
    xh = lax.rem(ctx // 2, 2)
    core = lax.rem(ctx, 2)

    def ctx_at(dz, dx, dc):
        return lax.rem(z + dz, 4) * 4 + lax.rem(xh + dx, 2) * 2 + lax.rem(core + dc, 2)

    def tp_at(dx):
        return lax.rem(tp + dx, 2)

    def samp_at(dy):
        return lax.rem(samp + dy, 4)

    def at(dz, dx, dc, dy=0):
        return {"ctx": ctx_at(dz, dx, dc), "samp": samp_at(dy), "tp": tp_at(dx)}

    def member(dy, dt):
        return {"samp": samp_at(dy), "tp": tp_at(dt)}

    barrier = pltpu.get_barrier_semaphore()
    for step in CTX_STEPS[:OWN]:
        pl.semaphore_signal(barrier, inc=1, device_id=at(*step), device_id_type=MESH)
    for dy, dt in MEMBERS:
        pl.semaphore_signal(barrier, inc=1, device_id=member(dy, dt), device_id_type=MESH)
    q_load = pltpu.make_async_copy(q_hbm, q_ref, load_sem.at[0])
    g_load = pltpu.make_async_copy(g_hbm, g_ref, load_sem.at[1])
    q_load.start()
    g_load.start()

    live = len_ref[0]
    tile = one_hot_tile(ap_ref[0])
    hot[OWN] = tile
    pl.semaphore_wait(barrier, OWN + len(MEMBERS))

    def hot_copy(k):
        return pltpu.make_async_remote_copy(
            src_ref=hot.at[OWN],
            dst_ref=hot.at[k],
            send_sem=hs.at[k],
            recv_sem=hr.at[k],
            device_id=at(*CTX_STEPS[k]),
            device_id_type=MESH,
        )

    for k in range(OWN):
        hot_copy(k).start()
    kt[:, PK:] = scaled_halves(akv_ref[:, :D]).T
    vt[:, PK:] = akv_ref[:, D:].T
    keys[PK:, :] = akv_ref[:, :D]
    q_load.wait()
    g_load.wait()

    def prepare_heads(i, carry):
        for h in range(4):
            prepare(4 * i + h, q_ref, g_ref, qt, gt, live)
        return carry

    lax.fori_loop(0, heads // 4, prepare_heads, 0)

    def pick_copy(k):
        return pltpu.make_async_remote_copy(
            src_ref=pick.at[k],
            dst_ref=chosen.at[ctx],
            send_sem=ps.at[k],
            recv_sem=pr.at[k],
            device_id=at(*CTX_STEPS[k]),
            device_id_type=MESH,
        )

    def choose(weights):
        total = pkv_ref[0].astype(F32) * weight_row(weights, 0)
        for p in range(1, NP):
            total = total + pkv_ref[p].astype(F32) * weight_row(weights, p)
        return total.astype(BF)

    def back(k):
        dz, dx, dc = CTX_STEPS[k]
        return CTX_STEPS.index(((4 - dz) % 4, dx, dc))

    for k in range(OWN):
        hot_copy(back(k)).wait_recv()
        pick[k] = choose(hot[back(k)])
        pick_copy(k).start()
    chosen[ctx] = choose(tile)

    def table_copy(i):
        return pltpu.make_async_remote_copy(
            src_ref=hot,
            dst_ref=hot_all.at[i],
            send_sem=ts.at[i],
            recv_sem=tr.at[i],
            device_id={"samp": samp_at(i)},
            device_id_type=MESH,
        )

    for i in (2, 1, 3):
        table_copy(i).start()

    def own_heads(i, carry):
        for h in range(4):
            own_products(4 * i + h, q_ref, g_ref, kt, vt, s_own, d_own, probs, dscores)
        return carry

    lax.fori_loop(0, heads // 4, own_heads, 0)

    def arrange(first_ctx):
        pair = jnp.concatenate([chosen[first_ctx], chosen[first_ctx + 1]], axis=0)
        start = pl.multiple_of(first_ctx * BL, 2 * BL)
        keys[pl.ds(start, 2 * BL), :] = pair[:, :D]
        kt[:, pl.ds(start, 2 * BL)] = scaled_halves(pair[:, :D]).T
        vt[:, pl.ds(start, 2 * BL)] = pair[:, D:].T

    for k in (14, 12, 4, 6, 8, 10, 0, 2):
        for one in (k, k + 1):
            if one != OWN:
                pick_copy(one).wait_recv()
        dz, dx, _ = CTX_STEPS[k]
        sender = lax.rem(z + 4 - dz, 4) * 4 + lax.rem(xh + dx, 2) * 2
        arrange(sender)

    products(0, q_ref, g_ref, kt, vt, s0, d0)

    def step(h, now, later):
        after = jnp.minimum(h + 1, heads - 1)
        products(after, q_ref, g_ref, kt, vt, *later)
        softmax_terms(h, *now, s_own, d_own, probs, dscores)

    buffers = ((s0, d0), (s1, d1))

    def some_heads(i, carry):
        for h in range(UNROLL):
            step(i * UNROLL + h, buffers[h % 2], buffers[(h + 1) % 2])
        return carry

    lax.fori_loop(0, heads // UNROLL, some_heads, 0)

    def piece_copy(k, i):
        dz, dx, dc = CTX_STEPS[k]
        row = ctx_at(dz, dx, dc) * BL + samp_at(i) * PIECE
        return pltpu.make_async_remote_copy(
            src_ref=grads.at[pl.ds(pl.multiple_of(row, PIECE), PIECE)],
            dst_ref=land.at[k, i],
            send_sem=bs.at[k, i],
            recv_sem=br.at[k, i],
            device_id=at(dz, dx, dc, i),
            device_id_type=MESH,
        )

    def key_value_grads(columns):
        key_grad = jnp.dot(qt[...], dscores[:, columns], preferred_element_type=F32) * SCALE
        value_grad = jnp.dot(gt[...], probs[:, columns], preferred_element_type=F32)
        return key_grad.T.astype(BF), value_grad.T.astype(BF)

    for first in range(0, OWN, 4):
        start = pl.multiple_of(lax.rem(z + CTX_STEPS[first][0], 4) * 256, 256)
        key_grad, value_grad = key_value_grads(pl.ds(start, 256))
        grads[pl.ds(start, 256), :D] = key_grad
        grads[pl.ds(start, 256), D:] = value_grad
        for k in range(first, first + 4):
            for i in SAMP_STEPS:
                if (k, i) != (OWN, 0):
                    piece_copy(k, i).start()
    row = pl.multiple_of(ctx * BL + samp * PIECE, PIECE)
    land[OWN, 0] = grads[pl.ds(row, PIECE), :]

    key_grad, value_grad = key_value_grads(slice(PK, NK))
    mine_kv[:, :D] = key_grad
    mine_kv[:, D:] = value_grad
    mate_copy = pltpu.make_async_remote_copy(
        src_ref=mine_kv,
        dst_ref=mate_kv,
        send_sem=xs,
        recv_sem=xr,
        device_id={"tp": 1 - tp},
        device_id_type=MESH,
    )
    mate_copy.start()

    groups = heads // GROUP
    width = GROUP * D

    def query_grads(i):
        rows = slice(i * GROUP * T, (i + 1) * GROUP * T)
        grad = jnp.dot(dscores[rows, :], keys[...], preferred_element_type=F32) * SCALE
        for h in range(GROUP):
            start = i * width + h * D
            dq[:, start : start + D] = grad[h * T : (h + 1) * T, :]

    for i in range(groups // 2):
        query_grads(i)
    for i in (2, 1, 3):
        table_copy(i).wait_recv()
    hot_all[0] = hot[...]
    sums = [jnp.zeros((PIECE, 2 * D), F32)] * NP
    for k in range(NC):
        for i in SAMP_STEPS:
            if (k, i) != (OWN, 0):
                piece_copy(k, i).wait_recv()
        for i in SAMP_STEPS:
            block = land[k, i].astype(F32)
            weights = hot_all[i, k]
            sums = [s + block * weight_row(weights, p) for p, s in enumerate(sums)]
    here = samp * 2 + tp
    for p in range(NP):
        part[p * PIECE : (p + 1) * PIECE, :] = sums[p].astype(BF)
    parts[here] = part[...]

    def part_copy(i):
        return pltpu.make_async_remote_copy(
            src_ref=part,
            dst_ref=parts.at[here],
            send_sem=ms.at[i],
            recv_sem=mr.at[i],
            device_id=member(*MEMBERS[i]),
            device_id_type=MESH,
        )

    for i in range(len(MEMBERS)):
        part_copy(i).start()
    for i in range(groups // 2, groups):
        query_grads(i)
    mate_copy.wait_recv()
    answer_out[...] = mine_kv[...].astype(F32) + mate_kv[...].astype(F32)
    for k in range(OWN):
        hot_copy(k).wait_send()
        pick_copy(k).wait_send()
    for i in (2, 1, 3):
        table_copy(i).wait_send()
    for k in range(NC):
        for i in SAMP_STEPS:
            if (k, i) != (OWN, 0):
                piece_copy(k, i).wait_send()
    mate_copy.wait_send()
    for i in range(len(MEMBERS)):
        part_copy(i).wait()
    for s in range(4):
        both = parts[2 * s].astype(F32) + parts[2 * s + 1].astype(F32)
        for p in range(NP):
            prompt_out[p, s * PIECE : (s + 1) * PIECE, :] = both[p * PIECE : (p + 1) * PIECE, :]


def backward(answer_len, answer_prompt, q, g, akv, pkv):
    heads = q.shape[1] // D
    rows = heads * T
    vmem = pltpu.VMEM
    dma = pltpu.SemaphoreType.DMA
    hbm = pl.BlockSpec(memory_space=pl.ANY)
    return pl.pallas_call(
        functools.partial(fused_kernel, heads),
        out_shape=(
            vmem((T, heads * D), F32),
            vmem((NP, BL, 2 * D), F32),
            vmem((T, 2 * D), F32),
        ),
        in_specs=[SM, SM, hbm, hbm, VM, VM],
        out_specs=(VM, VM, VM),
        scratch_shapes=[
            vmem((T, heads * D), BF),
            vmem((T, heads * D), BF),
            vmem((D, rows), BF),
            vmem((D, rows), BF),
            vmem((2 * D, NK), BF),
            vmem((D, NK), BF),
            vmem((NK, D), BF),
            vmem((T, PK), F32),
            vmem((heads, T, T), F32),
            vmem((heads, T, T), F32),
            vmem((rows, NK), BF),
            vmem((rows, NK), BF),
            vmem((NC, 8, 128), F32),
            vmem((4, NC, 8, 128), F32),
            vmem((OWN, BL, 2 * D), BF),
            vmem((NC, BL, 2 * D), BF),
            vmem((PK, 2 * D), BF),
            vmem((NC, 4, PIECE, 2 * D), BF),
            vmem((NP * PIECE, 2 * D), BF),
            vmem((NG, NP * PIECE, 2 * D), BF),
            vmem((T, 2 * D), BF),
            vmem((T, 2 * D), BF),
            dma((2,)),
            dma((NC,)), dma((NC,)), dma((NC,)), dma((NC,)),
            dma((4,)), dma((4,)),
            dma((NC, 4)), dma((NC, 4)),
            dma((NG,)), dma((NG,)),
            dma, dma,
        ],
        compiler_params=pltpu.CompilerParams(
            collective_id=0, has_side_effects=True, vmem_limit_bytes=57 * 2**20
        ),
        name="attention_backward",
    )(answer_len, answer_prompt, q, g, akv, pkv)


def place_kernel(*refs):
    count = len(refs) // 2
    ins, outs, sems = refs[:count], refs[count : 2 * count], refs[-1]
    copies = [pltpu.make_async_copy(ins[i], outs[i], sems.at[i]) for i in range(count)]
    for copy in copies:
        copy.start()
    for copy in copies:
        copy.wait()


def place(*arrays):
    hbm = pl.BlockSpec(memory_space=pl.ANY)
    return pl.pallas_call(
        place_kernel,
        out_shape=tuple(jax.ShapeDtypeStruct(a.shape, a.dtype) for a in arrays),
        in_specs=[VM] * len(arrays),
        out_specs=(hbm,) * len(arrays),
        scratch_shapes=[pltpu.SemaphoreType.DMA((len(arrays),))],
        compiler_params=pltpu.CompilerParams(vmem_limit_bytes=8 * 2**20),
        name="place_outputs",
    )(*arrays)


def body(queries, out_grad, answer_kv, prompt_kv, answer_prompt, answer_len):
    dq, prompt_grad, answer_grad = backward(
        answer_len, answer_prompt, queries[0], out_grad[0], answer_kv[0], prompt_kv
    )
    dq, answer_grad, prompt_grad = place(dq, answer_grad, prompt_grad)
    return dq[None], answer_grad[None], prompt_grad


def solution(mesh):
    placed = (
        P(("ctx", "samp"), None, "tp"),
        P(("ctx", "samp"), None, "tp"),
        P(("ctx", "samp"), None, None),
        P(None, "ctx", None),
        P(("ctx", "samp")),
        P(("ctx", "samp")),
    )
    return jax.shard_map(
        body,
        mesh=mesh,
        in_specs=placed,
        out_specs=(
            P(("ctx", "samp"), None, "tp"),
            P(("ctx", "samp"), None, None),
            P(None, "ctx", None),
        ),
        check_vma=False,
    )
```

```python
import functools

import jax
import jax.numpy as jnp
from jax import lax
from jax.experimental import pallas as pl
from jax.experimental.pallas import tpu as pltpu
from jax.sharding import PartitionSpec as P

BF = jnp.bfloat16
F32 = jnp.float32
T = 256
D = 128
PK = 1024
NK = PK + T
NP = 4
NC = 16
BL = PK // NC
NG = 8
SCALE = D**-0.5
EXP2 = SCALE * 1.4426950408889634
RC = 32
MESH = pl.DeviceIdType.MESH
VM = pl.BlockSpec(memory_space=pltpu.VMEM)
SM = pl.BlockSpec(memory_space=pltpu.SMEM)


def one_hot_tile(prompt):
    rows = lax.broadcasted_iota(jnp.int32, (8, 128), 0)
    return jnp.where(rows == prompt, 1.0, 0.0).astype(F32)


def weight_row(tile, prompt):
    row = tile[prompt : prompt + 1, :]
    return jnp.concatenate([row, row], axis=1)


def head_cols(h):
    return pl.ds(pl.multiple_of(h * D, D), D)


def head_rows(h):
    return pl.ds(pl.multiple_of(h * T, T), T)


def prepare(h, q_ref, g_ref, qt, gt, live):
    rows = lax.broadcasted_iota(jnp.int32, (T, D), 0)
    g = jnp.where(rows < live, g_ref[:, head_cols(h)].astype(F32), 0.0).astype(BF)
    g_ref[:, head_cols(h)] = g
    qt[:, head_rows(h)] = q_ref[:, head_cols(h)].T
    gt[:, head_rows(h)] = g.T


def scaled_halves(keys):
    scaled = keys.astype(F32) * EXP2
    high = scaled.astype(BF)
    low = (scaled - high.astype(F32)).astype(BF)
    return jnp.concatenate([high, low], axis=1)


def twice(q):
    return jnp.concatenate([q, q], axis=1)


def own_products(h, q_ref, g_ref, kt, vt, s_own, d_own, probs, dscores):
    s = jnp.dot(twice(q_ref[:, head_cols(h)]), kt[:, PK:], preferred_element_type=F32)
    row = lax.broadcasted_iota(jnp.int32, (T, T), 0)
    col = lax.broadcasted_iota(jnp.int32, (T, T), 1)
    s_own[h] = jnp.where(row >= col, s, -jnp.inf)
    d_own[h] = jnp.dot(g_ref[:, head_cols(h)], vt[:, PK:], preferred_element_type=F32)
    top_rows = pl.ds(pl.multiple_of(h * T, T), T // 2)
    probs[top_rows, PK + T // 2 :] = jnp.zeros((T // 2, T // 2), BF)
    dscores[top_rows, PK + T // 2 :] = jnp.zeros((T // 2, T // 2), BF)


def products(h, q_ref, g_ref, kt, vt, s_buf, d_buf):
    s_buf[...] = jnp.dot(twice(q_ref[:, head_cols(h)]), kt[:, :PK], preferred_element_type=F32)
    d_buf[...] = jnp.dot(g_ref[:, head_cols(h)], vt[:, :PK], preferred_element_type=F32)


def softmax_terms(h, s_buf, d_buf, s_own, d_own, probs, dscores):
    for r in range(T // RC):
        r0 = r * RC
        own = 128 if r0 < 128 else 256
        rows = slice(r0, r0 + RC)
        out_rows = pl.ds(pl.multiple_of(h * T + r0, RC), RC)
        s = jnp.concatenate([s_buf[rows, :], s_own[h, rows, :own]], axis=1)
        top = jnp.max(s, axis=1, keepdims=True)
        e = jnp.exp2(s - top)
        p = e * (1.0 / jnp.sum(e, axis=1, keepdims=True))
        probs[out_rows, : PK + own] = p.astype(BF)
        d = jnp.concatenate([d_buf[rows, :], d_own[h, rows, :own]], axis=1)
        delta = jnp.sum(p * d, axis=1, keepdims=True)
        dscores[out_rows, : PK + own] = (p * (d - delta)).astype(BF)


CTX_STEPS = [(dz, dx, dc) for dz in (2, 1, 3, 0) for dx in (1, 0) for dc in (1, 0)]
OWN = len(CTX_STEPS) - 1
SAMP_STEPS = (2, 1, 3, 0)
MEMBERS = [(dy, dt) for dy in (2, 1, 3, 0) for dt in (1, 0)][:-1]
UNROLL = 6
GROUP = 4
PIECE = BL // 4


def fused_kernel(
    heads, len_ref, ap_ref, q_hbm, g_hbm, akv_hbm, pkv_hbm,
    dq, prompt_out, answer_out,
    akv_ref, pkv_ref, q_ref, g_ref, qt, gt, kt, vt, keys, d1, s_own, d_own, probs, dscores,
    hot, hot_all, pick, chosen, grads, land, part, parts, mine_kv, mate_kv,
    load_sem, hs, hr, ps, pr, ts, tr, bs, br, ms, mr, xs, xr,
):
    s0, s1, d0 = (dq.at[:, pl.ds(i * PK, PK)] for i in range(3))
    ctx = lax.axis_index("ctx")
    samp = lax.axis_index("samp")
    tp = lax.axis_index("tp")
    z = ctx // 4
    xh = lax.rem(ctx // 2, 2)
    core = lax.rem(ctx, 2)

    def ctx_at(dz, dx, dc):
        return lax.rem(z + dz, 4) * 4 + lax.rem(xh + dx, 2) * 2 + lax.rem(core + dc, 2)

    def tp_at(dx):
        return lax.rem(tp + dx, 2)

    def samp_at(dy):
        return lax.rem(samp + dy, 4)

    def at(dz, dx, dc, dy=0):
        return {"ctx": ctx_at(dz, dx, dc), "samp": samp_at(dy), "tp": tp_at(dx)}

    def member(dy, dt):
        return {"samp": samp_at(dy), "tp": tp_at(dt)}

    barrier = pltpu.get_barrier_semaphore()
    for step in CTX_STEPS[:OWN]:
        pl.semaphore_signal(barrier, inc=1, device_id=at(*step), device_id_type=MESH)
    for dy, dt in MEMBERS:
        pl.semaphore_signal(barrier, inc=1, device_id=member(dy, dt), device_id_type=MESH)
    wanted = ((pkv_hbm, pkv_ref), (akv_hbm, akv_ref), (q_hbm, q_ref), (g_hbm, g_ref))
    loads = [pltpu.make_async_copy(*pair, load_sem.at[i]) for i, pair in enumerate(wanted)]
    for load in loads:
        load.start()
    live = len_ref[0]
    tile = one_hot_tile(ap_ref[0])
    hot[OWN] = tile
    pl.semaphore_wait(barrier, OWN + len(MEMBERS))

    def hot_copy(k):
        return pltpu.make_async_remote_copy(
            src_ref=hot.at[OWN],
            dst_ref=hot.at[k],
            send_sem=hs.at[k],
            recv_sem=hr.at[k],
            device_id=at(*CTX_STEPS[k]),
            device_id_type=MESH,
        )

    for k in range(OWN):
        hot_copy(k).start()
    loads[1].wait()
    kt[:, PK:] = scaled_halves(akv_ref[:, :D]).T
    vt[:, PK:] = akv_ref[:, D:].T
    keys[PK:, :] = akv_ref[:, :D]
    for load in loads[2:]:
        load.wait()

    def prepare_heads(i, carry):
        for h in range(4):
            prepare(4 * i + h, q_ref, g_ref, qt, gt, live)
        return carry

    lax.fori_loop(0, heads // 4, prepare_heads, 0)

    def pick_copy(k):
        return pltpu.make_async_remote_copy(
            src_ref=pick.at[k],
            dst_ref=chosen.at[ctx],
            send_sem=ps.at[k],
            recv_sem=pr.at[k],
            device_id=at(*CTX_STEPS[k]),
            device_id_type=MESH,
        )

    def choose(weights):
        total = pkv_ref[0] * weight_row(weights, 0).astype(BF)
        for p in range(1, NP):
            total = total + pkv_ref[p] * weight_row(weights, p).astype(BF)
        return total

    def back(k):
        dz, dx, dc = CTX_STEPS[k]
        return CTX_STEPS.index(((4 - dz) % 4, dx, dc))

    loads[0].wait()
    for k in reversed(range(OWN)):
        hot_copy(back(k)).wait_recv()
        pick[k] = choose(hot[back(k)])
        pick_copy(k).start()
    chosen[ctx] = choose(tile)

    def table_copy(i):
        return pltpu.make_async_remote_copy(
            src_ref=hot,
            dst_ref=hot_all.at[i],
            send_sem=ts.at[i],
            recv_sem=tr.at[i],
            device_id={"samp": samp_at(i)},
            device_id_type=MESH,
        )

    for i in (2, 1, 3):
        table_copy(i).start()

    def own_heads(i, carry):
        for h in range(4):
            own_products(4 * i + h, q_ref, g_ref, kt, vt, s_own, d_own, probs, dscores)
        return carry

    lax.fori_loop(0, heads // 4, own_heads, 0)

    def arrange(first_ctx):
        pair = jnp.concatenate([chosen[first_ctx], chosen[first_ctx + 1]], axis=0)
        start = pl.multiple_of(first_ctx * BL, 2 * BL)
        keys[pl.ds(start, 2 * BL), :] = pair[:, :D]
        kt[:, pl.ds(start, 2 * BL)] = scaled_halves(pair[:, :D]).T
        vt[:, pl.ds(start, 2 * BL)] = pair[:, D:].T

    for k in (14, 12, 4, 6, 8, 10, 0, 2):
        for one in (k, k + 1):
            if one != OWN:
                pick_copy(one).wait_recv()
        dz, dx, _ = CTX_STEPS[k]
        sender = lax.rem(z + 4 - dz, 4) * 4 + lax.rem(xh + dx, 2) * 2
        arrange(sender)

    products(0, q_ref, g_ref, kt, vt, s0, d0)

    def step(h, now, later):
        after = jnp.minimum(h + 1, heads - 1)
        products(after, q_ref, g_ref, kt, vt, *later)
        softmax_terms(h, *now, s_own, d_own, probs, dscores)

    buffers = ((s0, d0), (s1, d1))

    def some_heads(i, carry):
        for h in range(UNROLL):
            step(i * UNROLL + h, buffers[h % 2], buffers[(h + 1) % 2])
        return carry

    lax.fori_loop(0, heads // UNROLL, some_heads, 0)

    def piece_copy(k, i):
        dz, dx, dc = CTX_STEPS[k]
        row = ctx_at(dz, dx, dc) * BL + samp_at(i) * PIECE
        return pltpu.make_async_remote_copy(
            src_ref=grads.at[pl.ds(pl.multiple_of(row, PIECE), PIECE)],
            dst_ref=land.at[k, i],
            send_sem=bs.at[k, i],
            recv_sem=br.at[k, i],
            device_id=at(dz, dx, dc, i),
            device_id_type=MESH,
        )

    def key_value_grads(columns):
        key_grad = jnp.dot(qt[...], dscores[:, columns], preferred_element_type=F32) * SCALE
        value_grad = jnp.dot(gt[...], probs[:, columns], preferred_element_type=F32)
        return key_grad.T.astype(BF), value_grad.T.astype(BF)

    for first in range(0, OWN, 4):
        start = pl.multiple_of(lax.rem(z + CTX_STEPS[first][0], 4) * 256, 256)
        key_grad, value_grad = key_value_grads(pl.ds(start, 256))
        grads[pl.ds(start, 256), :D] = key_grad
        grads[pl.ds(start, 256), D:] = value_grad
        for k in range(first, first + 4):
            for i in SAMP_STEPS:
                if (k, i) != (OWN, 0):
                    piece_copy(k, i).start()
    row = pl.multiple_of(ctx * BL + samp * PIECE, PIECE)
    land[OWN, 0] = grads[pl.ds(row, PIECE), :]

    key_grad, value_grad = key_value_grads(slice(PK, NK))
    mine_kv[:, :D] = key_grad
    mine_kv[:, D:] = value_grad
    mate_copy = pltpu.make_async_remote_copy(
        src_ref=mine_kv,
        dst_ref=mate_kv,
        send_sem=xs,
        recv_sem=xr,
        device_id={"tp": 1 - tp},
        device_id_type=MESH,
    )
    mate_copy.start()

    groups = heads // GROUP

    def query_loop(i, carry):
        rows = pl.ds(pl.multiple_of(i * GROUP * T, GROUP * T), GROUP * T)
        grad = jnp.dot(dscores[rows, :], keys[...], preferred_element_type=F32) * SCALE
        for h in range(GROUP):
            dq[:, head_cols(i * GROUP + h)] = grad[h * T : (h + 1) * T, :]
        return carry

    lax.fori_loop(0, groups // 2, query_loop, 0)
    for i in (2, 1, 3):
        table_copy(i).wait_recv()
    hot_all[0] = hot[...]
    def piece_wait(k, i):
        return pltpu.make_async_remote_copy(
            src_ref=grads.at[pl.ds(0, PIECE)],
            dst_ref=land.at[k, i],
            send_sem=bs.at[k, i],
            recv_sem=br.at[k, i],
            device_id={"tp": 1 - tp},
            device_id_type=MESH,
        )

    def add_step(k, sums):
        for i in SAMP_STEPS:
            block = land[k, i].astype(F32)
            weights = hot_all[i, k]
            sums = tuple(s + block * weight_row(weights, p) for p, s in enumerate(sums))
        return sums

    def arrived(k, sums):
        for i in SAMP_STEPS:
            piece_wait(k, i).wait_recv()
        return add_step(k, sums)

    sums = (jnp.zeros((PIECE, 2 * D), F32),) * NP
    sums = lax.fori_loop(0, OWN, arrived, sums)
    for i in SAMP_STEPS[:-1]:
        piece_wait(OWN, i).wait_recv()
    sums = add_step(OWN, sums)
    here = samp * 2 + tp
    for p in range(NP):
        part[p * PIECE : (p + 1) * PIECE, :] = sums[p].astype(BF)
    parts[here] = part[...]

    def part_copy(i):
        return pltpu.make_async_remote_copy(
            src_ref=part,
            dst_ref=parts.at[here],
            send_sem=ms.at[i],
            recv_sem=mr.at[i],
            device_id=member(*MEMBERS[i]),
            device_id_type=MESH,
        )

    for i in range(len(MEMBERS)):
        part_copy(i).start()
    lax.fori_loop(groups // 2, groups, query_loop, 0)
    mate_copy.wait_recv()
    answer_out[...] = mine_kv[...].astype(F32) + mate_kv[...].astype(F32)
    for k in range(OWN):
        hot_copy(k).wait_send()
        pick_copy(k).wait_send()
    for i in (2, 1, 3):
        table_copy(i).wait_send()

    def sent(k, carry):
        for i in SAMP_STEPS:
            piece_wait(k, i).wait_send()
        return carry

    lax.fori_loop(0, OWN, sent, 0)
    for i in SAMP_STEPS[:-1]:
        piece_wait(OWN, i).wait_send()
    mate_copy.wait_send()
    for i in range(len(MEMBERS)):
        part_copy(i).wait()
    for s in range(4):
        both = parts[2 * s].astype(F32) + parts[2 * s + 1].astype(F32)
        for p in range(NP):
            prompt_out[p, s * PIECE : (s + 1) * PIECE, :] = both[p * PIECE : (p + 1) * PIECE, :]


def backward(answer_len, answer_prompt, q, g, akv, pkv):
    heads = q.shape[1] // D
    rows = heads * T
    vmem = pltpu.VMEM
    dma = pltpu.SemaphoreType.DMA
    hbm = pl.BlockSpec(memory_space=pl.ANY)
    return pl.pallas_call(
        functools.partial(fused_kernel, heads),
        out_shape=(
            vmem((T, heads * D), F32),
            vmem((NP, BL, 2 * D), F32),
            vmem((T, 2 * D), F32),
        ),
        in_specs=[SM, SM, hbm, hbm, hbm, hbm],
        out_specs=(VM, VM, VM),
        scratch_shapes=[
            vmem((T, 2 * D), BF),
            vmem((NP, BL, 2 * D), BF),
            vmem((T, heads * D), BF),
            vmem((T, heads * D), BF),
            vmem((D, rows), BF),
            vmem((D, rows), BF),
            vmem((2 * D, NK), BF),
            vmem((D, NK), BF),
            vmem((NK, D), BF),
            vmem((T, PK), F32),
            vmem((heads, T, T), F32),
            vmem((heads, T, T), F32),
            vmem((rows, NK), BF),
            vmem((rows, NK), BF),
            vmem((NC, 8, 128), F32),
            vmem((4, NC, 8, 128), F32),
            vmem((OWN, BL, 2 * D), BF),
            vmem((NC, BL, 2 * D), BF),
            vmem((PK, 2 * D), BF),
            vmem((NC, 4, PIECE, 2 * D), BF),
            vmem((NP * PIECE, 2 * D), BF),
            vmem((NG, NP * PIECE, 2 * D), BF),
            vmem((T, 2 * D), BF),
            vmem((T, 2 * D), BF),
            dma((4,)),
            dma((NC,)), dma((NC,)), dma((NC,)), dma((NC,)),
            dma((4,)), dma((4,)),
            dma((NC, 4)), dma((NC, 4)),
            dma((NG,)), dma((NG,)),
            dma, dma,
        ],
        compiler_params=pltpu.CompilerParams(
            collective_id=0, has_side_effects=True, vmem_limit_bytes=57 * 2**20
        ),
        name="attention_backward",
    )(answer_len, answer_prompt, q, g, akv, pkv)


def place_kernel(*refs):
    count = len(refs) // 2
    ins, outs, sems = refs[:count], refs[count : 2 * count], refs[-1]
    copies = [pltpu.make_async_copy(ins[i], outs[i], sems.at[i]) for i in range(count)]
    for copy in copies:
        copy.start()
    for copy in copies:
        copy.wait()


def place(*arrays):
    hbm = pl.BlockSpec(memory_space=pl.ANY)
    return pl.pallas_call(
        place_kernel,
        out_shape=tuple(jax.ShapeDtypeStruct(a.shape, a.dtype) for a in arrays),
        in_specs=[VM] * len(arrays),
        out_specs=(hbm,) * len(arrays),
        scratch_shapes=[pltpu.SemaphoreType.DMA((len(arrays),))],
        compiler_params=pltpu.CompilerParams(vmem_limit_bytes=8 * 2**20),
        name="place_outputs",
    )(*arrays)


def body(queries, out_grad, answer_kv, prompt_kv, answer_prompt, answer_len):
    dq, prompt_grad, answer_grad = backward(
        answer_len, answer_prompt, queries[0], out_grad[0], answer_kv[0], prompt_kv
    )
    dq, answer_grad, prompt_grad = place(dq, answer_grad, prompt_grad)
    return dq[None], answer_grad[None], prompt_grad


def solution(mesh):
    placed = (
        P(("ctx", "samp"), None, "tp"),
        P(("ctx", "samp"), None, "tp"),
        P(("ctx", "samp"), None, None),
        P(None, "ctx", None),
        P(("ctx", "samp")),
        P(("ctx", "samp")),
    )
    return jax.shard_map(
        body,
        mesh=mesh,
        in_specs=placed,
        out_specs=(
            P(("ctx", "samp"), None, "tp"),
            P(("ctx", "samp"), None, None),
            P(None, "ctx", None),
        ),
        check_vma=False,
    )
```

```python
import functools

import jax
import jax.numpy as jnp
from jax import lax
from jax.experimental import pallas as pl
from jax.experimental.pallas import tpu as pltpu
from jax.sharding import PartitionSpec as P

BF = jnp.bfloat16
F32 = jnp.float32
T = 256
D = 128
PK = 1024
NK = PK + T
NP = 4
NC = 16
BL = PK // NC
NG = 8
SCALE = D**-0.5
EXP2 = SCALE * 1.4426950408889634
RC = 32
MESH = pl.DeviceIdType.MESH
VM = pl.BlockSpec(memory_space=pltpu.VMEM)
SM = pl.BlockSpec(memory_space=pltpu.SMEM)


def one_hot_tile(prompt):
    rows = lax.broadcasted_iota(jnp.int32, (8, 128), 0)
    return jnp.where(rows == prompt, 1.0, 0.0).astype(F32)


def weight_row(tile, prompt):
    row = tile[prompt : prompt + 1, :]
    return jnp.concatenate([row, row], axis=1)


def head_cols(h):
    return pl.ds(pl.multiple_of(h * D, D), D)


def head_rows(h):
    return pl.ds(pl.multiple_of(h * T, T), T)


def prepare(h, q_ref, g_ref, qt, gt, live):
    rows = lax.broadcasted_iota(jnp.int32, (T, D), 0)
    g = jnp.where(rows < live, g_ref[:, head_cols(h)].astype(F32), 0.0).astype(BF)
    g_ref[:, head_cols(h)] = g
    qt[:, head_rows(h)] = q_ref[:, head_cols(h)].T
    gt[:, head_rows(h)] = g.T


def scaled_halves(keys):
    scaled = keys.astype(F32) * EXP2
    high = scaled.astype(BF)
    low = (scaled - high.astype(F32)).astype(BF)
    return jnp.concatenate([high, low], axis=1)


def twice(q):
    return jnp.concatenate([q, q], axis=1)


def own_products(h, q_ref, g_ref, kt, vt, s_own, d_own, probs, dscores):
    s = jnp.dot(twice(q_ref[:, head_cols(h)]), kt[:, PK:], preferred_element_type=F32)
    row = lax.broadcasted_iota(jnp.int32, (T, T), 0)
    col = lax.broadcasted_iota(jnp.int32, (T, T), 1)
    s_own[h] = jnp.where(row >= col, s, -jnp.inf)
    d_own[h] = jnp.dot(g_ref[:, head_cols(h)], vt[:, PK:], preferred_element_type=F32)
    top_rows = pl.ds(pl.multiple_of(h * T, T), T // 2)
    probs[top_rows, PK + T // 2 :] = jnp.zeros((T // 2, T // 2), BF)
    dscores[top_rows, PK + T // 2 :] = jnp.zeros((T // 2, T // 2), BF)


def products(h, q_ref, g_ref, kt, vt, s_buf, d_buf):
    s_buf[...] = jnp.dot(twice(q_ref[:, head_cols(h)]), kt[:, :PK], preferred_element_type=F32)
    d_buf[...] = jnp.dot(g_ref[:, head_cols(h)], vt[:, :PK], preferred_element_type=F32)


def softmax_terms(h, s_buf, d_buf, s_own, d_own, probs, dscores):
    for r in range(T // RC):
        r0 = r * RC
        own = 128 if r0 < 128 else 256
        rows = slice(r0, r0 + RC)
        out_rows = pl.ds(pl.multiple_of(h * T + r0, RC), RC)
        s = jnp.concatenate([s_buf[rows, :], s_own[h, rows, :own]], axis=1)
        top = jnp.max(s, axis=1, keepdims=True)
        e = jnp.exp2(s - top)
        p = e * (1.0 / jnp.sum(e, axis=1, keepdims=True))
        probs[out_rows, : PK + own] = p.astype(BF)
        d = jnp.concatenate([d_buf[rows, :], d_own[h, rows, :own]], axis=1)
        delta = jnp.sum(p * d, axis=1, keepdims=True)
        dscores[out_rows, : PK + own] = (p * (d - delta)).astype(BF)


CTX_STEPS = [(dz, dx, dc) for dz in (2, 1, 3, 0) for dx in (1, 0) for dc in (1, 0)]
OWN = len(CTX_STEPS) - 1
SAMP_STEPS = (2, 1, 3, 0)
MEMBERS = [(dy, dt) for dy in (2, 1, 3, 0) for dt in (1, 0)][:-1]
UNROLL = 6
GROUP = 4
PIECE = BL // 4


def fused_kernel(
    heads, len_ref, ap_ref, q_hbm, g_hbm, akv_hbm, pkv_hbm,
    dq, prompt_out, answer_out,
    akv_ref, pkv_ref, q_ref, g_ref, qt, gt, kt, vt, keys, d1, s_own, d_own, probs, dscores,
    hot, hot_all, pick, chosen, grads, land, part, parts, mine_kv, mate_kv,
    load_sem, hs, hr, ps, pr, ts, tr, bs, br, ms, mr, xs, xr,
):
    s0, s1, d0 = (dq.at[:, pl.ds(i * PK, PK)] for i in range(3))
    ctx = lax.axis_index("ctx")
    samp = lax.axis_index("samp")
    tp = lax.axis_index("tp")
    z = ctx // 4
    xh = lax.rem(ctx // 2, 2)
    core = lax.rem(ctx, 2)

    def ctx_at(dz, dx, dc):
        return lax.rem(z + dz, 4) * 4 + lax.rem(xh + dx, 2) * 2 + lax.rem(core + dc, 2)

    def tp_at(dx):
        return lax.rem(tp + dx, 2)

    def samp_at(dy):
        return lax.rem(samp + dy, 4)

    def at(dz, dx, dc, dy=0):
        return {"ctx": ctx_at(dz, dx, dc), "samp": samp_at(dy), "tp": tp_at(dx)}

    def member(dy, dt):
        return {"samp": samp_at(dy), "tp": tp_at(dt)}

    barrier = pltpu.get_barrier_semaphore()
    for step in CTX_STEPS[:OWN]:
        pl.semaphore_signal(barrier, inc=1, device_id=at(*step), device_id_type=MESH)
    for dy, dt in MEMBERS:
        pl.semaphore_signal(barrier, inc=1, device_id=member(dy, dt), device_id_type=MESH)
    wanted = ((pkv_hbm, pkv_ref), (akv_hbm, akv_ref), (q_hbm, q_ref), (g_hbm, g_ref))
    loads = [pltpu.make_async_copy(*pair, load_sem.at[i]) for i, pair in enumerate(wanted)]
    for load in loads:
        load.start()
    live = len_ref[0]
    tile = one_hot_tile(ap_ref[0])
    hot[OWN] = tile
    pl.semaphore_wait(barrier, OWN + len(MEMBERS))

    def hot_copy(k):
        return pltpu.make_async_remote_copy(
            src_ref=hot.at[OWN],
            dst_ref=hot.at[k],
            send_sem=hs.at[k],
            recv_sem=hr.at[k],
            device_id=at(*CTX_STEPS[k]),
            device_id_type=MESH,
        )

    for k in reversed(range(OWN)):
        hot_copy(k).start()
    loads[1].wait()
    kt[:, PK:] = scaled_halves(akv_ref[:, :D]).T
    vt[:, PK:] = akv_ref[:, D:].T
    keys[PK:, :] = akv_ref[:, :D]
    for load in loads[2:]:
        load.wait()

    def prepare_heads(i, carry):
        for h in range(4):
            prepare(4 * i + h, q_ref, g_ref, qt, gt, live)
        return carry

    lax.fori_loop(0, heads // 4, prepare_heads, 0)

    def pick_copy(k):
        return pltpu.make_async_remote_copy(
            src_ref=pick.at[k],
            dst_ref=chosen.at[ctx],
            send_sem=ps.at[k],
            recv_sem=pr.at[k],
            device_id=at(*CTX_STEPS[k]),
            device_id_type=MESH,
        )

    def choose(weights):
        total = pkv_ref[0] * weight_row(weights, 0).astype(BF)
        for p in range(1, NP):
            total = total + pkv_ref[p] * weight_row(weights, p).astype(BF)
        return total

    def back(k):
        dz, dx, dc = CTX_STEPS[k]
        return CTX_STEPS.index(((4 - dz) % 4, dx, dc))

    loads[0].wait()
    for k in reversed(range(OWN)):
        hot_copy(back(k)).wait_recv()
        pick[k] = choose(hot[back(k)])
        pick_copy(k).start()
    chosen[ctx] = choose(tile)

    def table_copy(i):
        return pltpu.make_async_remote_copy(
            src_ref=hot,
            dst_ref=hot_all.at[i],
            send_sem=ts.at[i],
            recv_sem=tr.at[i],
            device_id={"samp": samp_at(i)},
            device_id_type=MESH,
        )


    def own_heads(i, carry):
        for h in range(4):
            own_products(4 * i + h, q_ref, g_ref, kt, vt, s_own, d_own, probs, dscores)
        return carry

    lax.fori_loop(0, heads // 4, own_heads, 0)

    def arrange(first_ctx):
        pair = jnp.concatenate([chosen[first_ctx], chosen[first_ctx + 1]], axis=0)
        start = pl.multiple_of(first_ctx * BL, 2 * BL)
        keys[pl.ds(start, 2 * BL), :] = pair[:, :D]
        kt[:, pl.ds(start, 2 * BL)] = scaled_halves(pair[:, :D]).T
        vt[:, pl.ds(start, 2 * BL)] = pair[:, D:].T

    for k in (14, 12, 4, 6, 8, 10, 0, 2):
        for one in (k, k + 1):
            if one != OWN:
                pick_copy(one).wait_recv()
        dz, dx, _ = CTX_STEPS[k]
        sender = lax.rem(z + 4 - dz, 4) * 4 + lax.rem(xh + dx, 2) * 2
        arrange(sender)

    for i in (2, 1, 3):
        table_copy(i).start()
    products(0, q_ref, g_ref, kt, vt, s0, d0)

    def step(h, now, later):
        after = jnp.minimum(h + 1, heads - 1)
        products(after, q_ref, g_ref, kt, vt, *later)
        softmax_terms(h, *now, s_own, d_own, probs, dscores)

    buffers = ((s0, d0), (s1, d1))

    def some_heads(i, carry):
        for h in range(UNROLL):
            step(i * UNROLL + h, buffers[h % 2], buffers[(h + 1) % 2])
        return carry

    lax.fori_loop(0, heads // UNROLL, some_heads, 0)

    def piece_copy(k, i):
        dz, dx, dc = CTX_STEPS[k]
        row = ctx_at(dz, dx, dc) * BL + samp_at(i) * PIECE
        return pltpu.make_async_remote_copy(
            src_ref=grads.at[pl.ds(pl.multiple_of(row, PIECE), PIECE)],
            dst_ref=land.at[k, i],
            send_sem=bs.at[k, i],
            recv_sem=br.at[k, i],
            device_id=at(dz, dx, dc, i),
            device_id_type=MESH,
        )

    def key_value_grads(columns):
        key_grad = jnp.dot(qt[...], dscores[:, columns], preferred_element_type=F32) * SCALE
        value_grad = jnp.dot(gt[...], probs[:, columns], preferred_element_type=F32)
        return key_grad.T.astype(BF), value_grad.T.astype(BF)

    for first in (4, 0, 8, 12):
        start = pl.multiple_of(lax.rem(z + CTX_STEPS[first][0], 4) * 256, 256)
        key_grad, value_grad = key_value_grads(pl.ds(start, 256))
        grads[pl.ds(start, 256), :D] = key_grad
        grads[pl.ds(start, 256), D:] = value_grad
        for k in range(first, first + 4):
            for i in SAMP_STEPS:
                if (k, i) != (OWN, 0):
                    piece_copy(k, i).start()
    row = pl.multiple_of(ctx * BL + samp * PIECE, PIECE)
    land[OWN, 0] = grads[pl.ds(row, PIECE), :]

    key_grad, value_grad = key_value_grads(slice(PK, NK))
    mine_kv[:, :D] = key_grad
    mine_kv[:, D:] = value_grad
    mate_copy = pltpu.make_async_remote_copy(
        src_ref=mine_kv,
        dst_ref=mate_kv,
        send_sem=xs,
        recv_sem=xr,
        device_id={"tp": 1 - tp},
        device_id_type=MESH,
    )
    mate_copy.start()

    groups = heads // GROUP

    def query_loop(i, carry):
        rows = pl.ds(pl.multiple_of(i * GROUP * T, GROUP * T), GROUP * T)
        grad = jnp.dot(dscores[rows, :], keys[...], preferred_element_type=F32) * SCALE
        for h in range(GROUP):
            dq[:, head_cols(i * GROUP + h)] = grad[h * T : (h + 1) * T, :]
        return carry

    lax.fori_loop(0, groups // 2, query_loop, 0)
    for i in (2, 1, 3):
        table_copy(i).wait_recv()
    hot_all[0] = hot[...]
    def piece_wait(k, i):
        return pltpu.make_async_remote_copy(
            src_ref=grads.at[pl.ds(0, PIECE)],
            dst_ref=land.at[k, i],
            send_sem=bs.at[k, i],
            recv_sem=br.at[k, i],
            device_id={"tp": 1 - tp},
            device_id_type=MESH,
        )

    def add_step(k, sums):
        for i in SAMP_STEPS:
            block = land[k, i].astype(F32)
            weights = hot_all[i, k]
            sums = tuple(s + block * weight_row(weights, p) for p, s in enumerate(sums))
        return sums

    def arrived(k, sums):
        for i in SAMP_STEPS:
            piece_wait(k, i).wait_recv()
        return add_step(k, sums)

    sums = (jnp.zeros((PIECE, 2 * D), F32),) * NP
    sums = lax.fori_loop(0, OWN, arrived, sums)
    for i in SAMP_STEPS[:-1]:
        piece_wait(OWN, i).wait_recv()
    sums = add_step(OWN, sums)
    here = samp * 2 + tp
    for p in range(NP):
        part[p * PIECE : (p + 1) * PIECE, :] = sums[p].astype(BF)
    parts[here] = part[...]

    def part_copy(i):
        return pltpu.make_async_remote_copy(
            src_ref=part,
            dst_ref=parts.at[here],
            send_sem=ms.at[i],
            recv_sem=mr.at[i],
            device_id=member(*MEMBERS[i]),
            device_id_type=MESH,
        )

    for i in range(len(MEMBERS)):
        part_copy(i).start()
    lax.fori_loop(groups // 2, groups, query_loop, 0)
    mate_copy.wait_recv()
    answer_out[...] = mine_kv[...].astype(F32) + mate_kv[...].astype(F32)
    for k in range(OWN):
        hot_copy(k).wait_send()
        pick_copy(k).wait_send()
    for i in (2, 1, 3):
        table_copy(i).wait_send()

    def sent(k, carry):
        for i in SAMP_STEPS:
            piece_wait(k, i).wait_send()
        return carry

    lax.fori_loop(0, OWN, sent, 0)
    for i in SAMP_STEPS[:-1]:
        piece_wait(OWN, i).wait_send()
    mate_copy.wait_send()
    for i in range(len(MEMBERS)):
        part_copy(i).wait()
    for s in range(4):
        both = parts[2 * s].astype(F32) + parts[2 * s + 1].astype(F32)
        for p in range(NP):
            prompt_out[p, s * PIECE : (s + 1) * PIECE, :] = both[p * PIECE : (p + 1) * PIECE, :]


def backward(answer_len, answer_prompt, q, g, akv, pkv):
    heads = q.shape[1] // D
    rows = heads * T
    vmem = pltpu.VMEM
    dma = pltpu.SemaphoreType.DMA
    hbm = pl.BlockSpec(memory_space=pl.ANY)
    return pl.pallas_call(
        functools.partial(fused_kernel, heads),
        out_shape=(
            vmem((T, heads * D), F32),
            vmem((NP, BL, 2 * D), F32),
            vmem((T, 2 * D), F32),
        ),
        in_specs=[SM, SM, hbm, hbm, hbm, hbm],
        out_specs=(VM, VM, VM),
        scratch_shapes=[
            vmem((T, 2 * D), BF),
            vmem((NP, BL, 2 * D), BF),
            vmem((T, heads * D), BF),
            vmem((T, heads * D), BF),
            vmem((D, rows), BF),
            vmem((D, rows), BF),
            vmem((2 * D, NK), BF),
            vmem((D, NK), BF),
            vmem((NK, D), BF),
            vmem((T, PK), F32),
            vmem((heads, T, T), F32),
            vmem((heads, T, T), F32),
            vmem((rows, NK), BF),
            vmem((rows, NK), BF),
            vmem((NC, 8, 128), F32),
            vmem((4, NC, 8, 128), F32),
            vmem((OWN, BL, 2 * D), BF),
            vmem((NC, BL, 2 * D), BF),
            vmem((PK, 2 * D), BF),
            vmem((NC, 4, PIECE, 2 * D), BF),
            vmem((NP * PIECE, 2 * D), BF),
            vmem((NG, NP * PIECE, 2 * D), BF),
            vmem((T, 2 * D), BF),
            vmem((T, 2 * D), BF),
            dma((4,)),
            dma((NC,)), dma((NC,)), dma((NC,)), dma((NC,)),
            dma((4,)), dma((4,)),
            dma((NC, 4)), dma((NC, 4)),
            dma((NG,)), dma((NG,)),
            dma, dma,
        ],
        compiler_params=pltpu.CompilerParams(
            collective_id=0, has_side_effects=True, vmem_limit_bytes=57 * 2**20
        ),
        name="attention_backward",
    )(answer_len, answer_prompt, q, g, akv, pkv)


def place_kernel(*refs):
    count = len(refs) // 2
    ins, outs, sems = refs[:count], refs[count : 2 * count], refs[-1]
    copies = [pltpu.make_async_copy(ins[i], outs[i], sems.at[i]) for i in range(count)]
    for copy in copies:
        copy.start()
    for copy in copies:
        copy.wait()


def place(*arrays):
    hbm = pl.BlockSpec(memory_space=pl.ANY)
    return pl.pallas_call(
        place_kernel,
        out_shape=tuple(jax.ShapeDtypeStruct(a.shape, a.dtype) for a in arrays),
        in_specs=[VM] * len(arrays),
        out_specs=(hbm,) * len(arrays),
        scratch_shapes=[pltpu.SemaphoreType.DMA((len(arrays),))],
        compiler_params=pltpu.CompilerParams(vmem_limit_bytes=8 * 2**20),
        name="place_outputs",
    )(*arrays)


def body(queries, out_grad, answer_kv, prompt_kv, answer_prompt, answer_len):
    dq, prompt_grad, answer_grad = backward(
        answer_len, answer_prompt, queries[0], out_grad[0], answer_kv[0], prompt_kv
    )
    dq, answer_grad, prompt_grad = place(dq, answer_grad, prompt_grad)
    return dq[None], answer_grad[None], prompt_grad


def solution(mesh):
    placed = (
        P(("ctx", "samp"), None, "tp"),
        P(("ctx", "samp"), None, "tp"),
        P(("ctx", "samp"), None, None),
        P(None, "ctx", None),
        P(("ctx", "samp")),
        P(("ctx", "samp")),
    )
    return jax.shard_map(
        body,
        mesh=mesh,
        in_specs=placed,
        out_specs=(
            P(("ctx", "samp"), None, "tp"),
            P(("ctx", "samp"), None, None),
            P(None, "ctx", None),
        ),
        check_vma=False,
    )
```
